128 devices in a mesh: row: 16 (over z, y), col: 8 (over x, core).
Axes of the slice: x: 4, y: 4, z: 4, core: 2. Of those that a mesh axis runs over, the one named last changes fastest.
Arguments:
- amplitudes: bfloat16 [8192, 7680], P(('row', 'col')), may hold values from -6 to 6
- integrals: bfloat16 [8, 7680, 1920], P('col', 'row'), may hold values from -0.0625 to 0.0625
- tile_ids: int32 [80], replicated, may hold values from 0 to 42335, as said below
- tile_owner: int32 [80], replicated, may hold values from 0 to 7, as said below
- occ_pairs: int32 [8192, 2], replicated, may hold values from 0 to 199
- occ_energy: float32 [200], replicated, may hold values from -1 to -0.2
- vir_energy: float32 [2016], replicated, may hold values from 0.1 to 1.5
Outputs:
- ladder_update: float32 [16, 512, 7680], P('row', 'col')
The draws below stay inside these ranges and needn't reach their ends.
Inputs may be any that keep to these rules, and one draw needn't show every extreme that they name: `tile_ids`: distinct; tile g covers the flat virtual pairs g * 96 to g * 96 + 95, flat pair f being the virtuals f // 2016 and f % 2016. `tile_owner`: every column owns at least one tile and at most 20, one column exactly 20; integral slots past a column's count are unused.
All inputs are finite; a program needn't handle non-finite values.
Results may differ from the reference program's by a relative error of at most 0.0003.
Values may be sent and summed in bfloat16 or wider, within the bound.
No kernel may reach another device: no remote copies, remote signals or barrier semaphores. Data moves between devices by JAX's collectives and lax.ppermute only.
A program may use at most 128 MiB of HBM per device.

```python
import jax
import jax.numpy as jnp

TW = 96
NVIR = 2016
NOCC = 200
K = 80
OCC_DEV = 64
NPAIR = 8192
CAP = 20
SUB = 4
N_ROW = 16
N_COL = 8


def draw_tile_ids(key, part):
    key = jax.random.fold_in(key, 11)
    shuffled = jax.random.permutation(key, NVIR * NVIR // TW)
    return shuffled[:K].astype(jnp.int32)


def draw_tile_owner(key, part):
    key = jax.random.fold_in(key, 23)
    first_key, second_key = jax.random.split(key)
    busiest = jax.random.randint(first_key, (), 0, N_COL)
    positions = jnp.arange(K, dtype=jnp.int32)
    spread_cols = (busiest + 1 + (positions - CAP) % (N_COL - 1)) % N_COL
    col_sequence = jnp.where(positions < CAP, busiest, spread_cols).astype(jnp.int32)
    shuffled = jax.random.permutation(second_key, K)
    return jnp.zeros((K,), jnp.int32).at[shuffled].set(col_sequence)


def place_ends(result, stream_key, smallest, high):
    longest = result.shape.index(max(result.shape))
    spots = []
    for shift in (0, 1):
        where = [jax.random.randint(jax.random.fold_in(stream_key, axis), (), 0, length) for axis, length in enumerate(result.shape)]
        where[longest] = (where[longest] + shift) % result.shape[longest]
        spots.append(tuple(where))
    return result.at[spots[0]].set(smallest).at[spots[1]].set(high)


def block_levels(rng, dims, shards, low, top_value):
    def one(axis_at, blocks):
        heights = jax.random.uniform(jax.random.fold_in(jax.random.fold_in(rng, 6), axis_at), (blocks,), jnp.float32, low / len(shards), top_value / len(shards))
        return jnp.repeat(jnp.exp(heights), dims[axis_at] // blocks).reshape((-1,) + (1,) * (len(dims) - axis_at - 1))

    factor_of = one(*shards[0])
    for cut in shards[1:]:
        factor_of = factor_of * one(*cut)
    return factor_of


def centred(rng, dims, scale, bound, pieces=(), kind=jnp.bfloat16):
    result = jax.random.normal(rng, dims, jnp.float32) * scale
    if len(pieces) > 0:
        result = block_levels(rng, dims, pieces, -0.22, 0.18) * result
    return jnp.clip(result, min=-bound, max=bound).astype(kind)


def setup_inputs(seed: int = 0) -> dict:
    splits = jax.random.split(jax.random.key(seed), 8)
    return {
        "amplitudes": centred(splits[0], (NPAIR, K * TW), 1.0, 6.0, ((0, 128),)),
        "integrals": centred(splits[1], (N_COL, K * TW, CAP * TW), (K * TW) ** -0.5, 0.0625, ((0, 8), (1, 16))),
        "tile_ids": draw_tile_ids(jax.random.fold_in(splits[7], 71), 0),
        "tile_owner": draw_tile_owner(jax.random.fold_in(splits[7], 71), 0),
        "occ_pairs": place_ends(jax.random.randint(splits[4], (NPAIR, 2), 0, NOCC), jax.random.fold_in(splits[4], 1), 0, NOCC - 1).astype(jnp.int32),
        "occ_energy": jnp.clip(jax.random.uniform(splits[5], (NOCC,), jnp.float32, -1.0, -0.2), -1.0, -0.2),
        "vir_energy": jnp.clip(jax.random.uniform(splits[6], (NVIR,), jnp.float32, 0.1, 1.5), 0.1, 1.5),
    }


def slot_table(tile_owner):
    positions = jnp.arange(tile_owner.shape[0])
    same_col = tile_owner[:, None] == tile_owner[None, :]
    earlier = positions[None, :] < positions[:, None]
    return jnp.sum(jnp.logical_and(same_col, earlier), axis=1).astype(jnp.int32)


def reference(amplitudes, integrals, tile_ids, tile_owner, occ_pairs, occ_energy, vir_energy):
    slot_index = slot_table(tile_owner)
    tile_rows = integrals.reshape(N_COL, K * TW, CAP, TW)[tile_owner, :, slot_index, :]
    full_rows = jnp.transpose(tile_rows, (0, 2, 1)).reshape(K * TW, K * TW)
    residual = jnp.dot(amplitudes, full_rows, preferred_element_type=jnp.float32)
    flat_pair = tile_ids[:, None] * TW + jnp.arange(TW, dtype=jnp.int32)[None, :]
    virt_sum = (vir_energy[flat_pair // NVIR] + vir_energy[flat_pair % NVIR]).reshape(K * TW)
    occ_sum = occ_energy[occ_pairs[:, 0]] + occ_energy[occ_pairs[:, 1]]
    update = residual / (virt_sum[None, :] - occ_sum[:, None])
    update = update.reshape(N_ROW, N_COL, N_ROW, SUB, K * TW)
    update = jnp.transpose(update, (2, 1, 0, 3, 4))
    return update.reshape(N_ROW, N_COL * OCC_DEV, K * TW)
```

```python
import jax
import jax.numpy as jnp
from jax import lax
from jax.sharding import Mesh, PartitionSpec as P

TW = 96
NVIR = 2016
SIDE = 4
CHIP_TILES = 20
ROUND_TILES = 4
ALL = ("z", "y", "x", "c")


def ring(value, axis, shift):
    return lax.ppermute(value, axis, [(i, (i + shift) % SIDE) for i in range(SIDE)])


def swap(value):
    return lax.ppermute(value, "c", [(0, 1), (1, 0)])


def assignment(tile_owner):
    count = tile_owner.shape[0]
    ids = jnp.arange(count, dtype=jnp.int32)
    chips = jnp.arange(SIDE, dtype=jnp.int32)
    earlier = ids[None, :] < ids[:, None]
    slot = jnp.sum((tile_owner[:, None] == tile_owner[None, :]) & earlier, axis=1, dtype=jnp.int32)
    home = tile_owner // 2
    rank = jnp.sum((home[:, None] == home[None, :]) & earlier, axis=1, dtype=jnp.int32)
    load = jnp.sum(home[:, None] == chips[None, :], axis=0, dtype=jnp.int32)
    over = jnp.maximum(load - CHIP_TILES, 0)
    under = jnp.maximum(CHIP_TILES - load, 0)
    lower = chips[None, :] < chips[:, None]
    over_before = jnp.sum(jnp.where(lower, over[None, :], 0), axis=1)
    under_before = jnp.sum(jnp.where(lower, under[None, :], 0), axis=1)
    is_home = home[:, None] == chips[None, :]
    at_home = lambda table: jnp.sum(jnp.where(is_home, table[None, :], 0), axis=1)
    moves = rank >= CHIP_TILES
    number = at_home(over_before) + rank - CHIP_TILES
    target = jnp.sum(number[:, None] >= (under_before + under)[None, :], axis=1, dtype=jnp.int32)
    target = jnp.where(moves, target, home)
    is_target = target[:, None] == chips[None, :]
    start = jnp.sum(jnp.where(is_target, (load - under_before)[None, :], 0), axis=1)
    pos = jnp.where(moves, start + number, rank)
    same = moves[None, :] & (home[:, None] == home[None, :]) & (target[:, None] == target[None, :])
    order = jnp.sum(same & earlier, axis=1, dtype=jnp.int32)
    return slot, home, moves, target, pos, order


def invert(keys, size, values):
    hit = keys[None, :] == jnp.arange(size, dtype=jnp.int32)[:, None]
    return jnp.sum(jnp.where(hit, values[None, :], 0), axis=1, dtype=jnp.int32)


def on_device(amplitudes, integrals, tile_ids, tile_owner, occ_pairs, occ_energy, vir_energy):
    z, y, x, c = (lax.axis_index(name) for name in ALL)
    occ_dev = amplitudes.shape[0]
    kept = tile_ids.shape[0]
    local = integrals[0]
    rows, depth = local.shape
    slots = depth // TW
    half = rows // 2
    sub = occ_dev // (SIDE * SIDE)
    width = CHIP_TILES * TW

    slot, home, moves, target, pos, order = assignment(tile_owner)

    keep_rows = lax.dynamic_slice_in_dim(local, c * half, half, axis=0)
    send_rows = lax.dynamic_slice_in_dim(local, (1 - c) * half, half, axis=0)
    both = jnp.concatenate([keep_rows, swap(send_rows)], axis=1).reshape(half, 2 * slots, TW)
    place = jnp.where(tile_owner % 2 == c, slot, slots + slot)
    leaving = moves & (home == x)
    shift = (target - home) % SIDE
    key = jnp.where(leaving, (shift - 1) * CHIP_TILES + order, -1)
    outgoing = invert(key, 3 * CHIP_TILES, place).reshape(3, CHIP_TILES)
    mine = target == x
    source = jnp.where(moves, 2 * slots + (shift - 1) * CHIP_TILES + order, place)
    gather_from = invert(jnp.where(mine, pos, -1), CHIP_TILES, source)
    rounds = (jnp.max(jnp.where(moves, order, -1)) + ROUND_TILES) // ROUND_TILES

    def exchange(number, received):
        parts = []
        for s in range(3):
            pick = lax.dynamic_slice_in_dim(outgoing[s], number * ROUND_TILES, ROUND_TILES)
            parts.append(ring(jnp.take(both, pick, axis=1).reshape(half, ROUND_TILES * TW), "x", s + 1))
        block = jnp.stack(parts).reshape(3, half, ROUND_TILES, TW)
        return lax.dynamic_update_slice(received, block, (0, 0, number * ROUND_TILES, 0))

    received = exchange(jnp.int32(0), jnp.zeros((3, half, CHIP_TILES, TW), local.dtype))
    received = lax.fori_loop(1, jnp.maximum(rounds, 1), exchange, received)
    pool = jnp.concatenate([both] + [received[s] for s in range(3)], axis=1)
    shard = jnp.take(pool, gather_from, axis=1).reshape(half, width)

    from_low = ring(shard, "y", 1)
    from_high = ring(shard, "y", -1)
    far = jnp.concatenate(
        [ring(from_low[: half // 2], "y", 1), ring(from_high[half // 2 :], "y", -1)], axis=0
    )
    block = jnp.zeros((SIDE * rows, width), local.dtype)
    for piece, where in ((shard, y), (from_low, y + 3), (from_high, y + 1), (far, y + 2)):
        first = (where % SIDE) * rows
        block = lax.dynamic_update_slice(block, piece, (first + c * half, 0))
        block = lax.dynamic_update_slice(block, swap(piece), (first + (1 - c) * half, 0))

    perm = invert(target * CHIP_TILES + pos, kept, jnp.arange(kept, dtype=jnp.int32))
    taken = jnp.take(amplitudes.reshape(occ_dev, kept, TW), perm, axis=1)
    taken = taken.reshape(SIDE, SIDE, sub, SIDE, width)
    taken = jnp.transpose(taken, (1, 3, 0, 2, 4)).reshape(SIDE * SIDE, SIDE * sub, width)
    arrived = lax.all_to_all(taken, ("y", "x"), split_axis=0, concat_axis=0, tiled=True)
    arrived = arrived.reshape(SIDE, SIDE, SIDE * sub, width)

    def pairs_of(xo):
        piece = lax.dynamic_index_in_dim(arrived, xo % SIDE, axis=1, keepdims=False)
        piece = piece.reshape(occ_dev, width)
        low = ring(piece, "z", 1)
        high = ring(piece, "z", -1)
        cut = occ_dev // 2
        far = jnp.concatenate([ring(low[:cut], "z", 1), ring(high[cut:], "z", -1)], axis=0)
        out = jnp.zeros((SIDE, occ_dev, width), piece.dtype)
        for part, where in ((piece, z), (low, z + 3), (high, z + 1), (far, z + 2)):
            out = lax.dynamic_update_slice(out, part[None], (where % SIDE, 0, 0))
        return out.reshape(SIDE * occ_dev, width)

    def partial(xo):
        return lax.dot_general(
            pairs_of(xo), block, (((1,), (1,)), ((), ())), preferred_element_type=jnp.float32
        )

    cut = 2 * occ_dev
    across = partial(x + 2)
    up = ring(across[:cut], "x", 1)
    down = ring(across[cut:], "x", -1)
    nxt = partial(x + 1)
    prv = partial(x + 3)
    from_low = ring(jnp.concatenate([nxt[:cut] + up, nxt[cut:]], axis=0), "x", 1)
    from_high = ring(jnp.concatenate([prv[:cut], prv[cut:] + down], axis=0), "x", -1)
    total = partial(x) + from_low + from_high

    total = total.reshape(SIDE * SIDE, SIDE, sub, SIDE * rows)
    total = jnp.transpose(total, (1, 0, 2, 3)).reshape(SIDE, occ_dev, SIDE * rows)
    residual = lax.all_to_all(total, "z", split_axis=0, concat_axis=0, tiled=True)
    residual = jnp.transpose(residual.reshape(SIDE, occ_dev, SIDE * rows), (1, 0, 2))
    residual = residual.reshape(occ_dev, kept * TW)

    grid = occ_pairs.reshape(SIDE * SIDE, 2 * SIDE, SIDE * SIDE, sub, 2)
    here = lax.dynamic_slice(grid, (0, 2 * x + c, SIDE * z + y, 0, 0), (SIDE * SIDE, 1, 1, sub, 2))
    occ_sum = jnp.sum(jnp.take(occ_energy, here.reshape(occ_dev, 2), axis=0), axis=1)
    per_row = NVIR // TW
    second = jnp.take(vir_energy.reshape(per_row, TW), tile_ids % per_row, axis=0)
    virt_sum = (jnp.take(vir_energy, tile_ids // per_row)[:, None] + second).reshape(kept * TW)
    update = residual / (virt_sum[None, :] - occ_sum[:, None])
    return update[None]


def solution(mesh):
    chips = Mesh(mesh.devices.reshape(SIDE, SIDE, SIDE, 2), ALL)
    placed = (P(ALL, None), P(("x", "c"), ("z", "y"), None), P(), P(), P(), P(), P())
    return jax.shard_map(
        on_device, mesh=chips, in_specs=placed, out_specs=P(("z", "y"), ("x", "c"), None), check_vma=False
    )
```

```python
import functools

import jax
import jax.numpy as jnp
from jax import lax
from jax.experimental import pallas as pl
from jax.experimental.pallas import tpu as pltpu
from jax.sharding import Mesh, PartitionSpec as P

TW = 96
NVIR = 2016
SIDE = 4
TILES = 80
CAP = 20
QUAD = 4
LANES = 128
WINDOW = 2 * LANES
HALF = 240
PADDED = 256
WIDTH = CAP * TW
CUT = 128
LEVELS = 32000.0
STEPS = 256.0
ALL = ("z", "y", "x", "c")
SEND = 0
GATHER = 3 * CAP
ROUNDS = GATHER + CAP
VMEM = pltpu.CompilerParams(vmem_limit_bytes=48 * 1024 * 1024)


def ring(value, axis, shift):
    return lax.ppermute(value, axis, [(i, (i + shift) % SIDE) for i in range(SIDE)])


def swap(value):
    return lax.ppermute(value, "c", [(0, 1), (1, 0)])


def four_tiles(load, starts, limit):
    parts = []
    for start, want in zip(starts, (0, 96, 64, 160)):
        base = jnp.minimum((start // LANES) * LANES, limit - WINDOW)
        window = load(pl.multiple_of(base, LANES))
        parts.append(pltpu.roll(window, (want - (start - base)) & (WINDOW - 1), 1))
    a, b, c, d = parts
    lane = lax.broadcasted_iota(jnp.int32, (a.shape[0], LANES), 1)
    return (
        jnp.where(lane < 96, a[:, :LANES], b[:, :LANES]),
        jnp.where(lane < 64, b[:, LANES:], c[:, :LANES]),
        jnp.where(lane < 32, c[:, LANES:], d[:, LANES:]),
    )


def one_hot(size, source):
    row = lax.broadcasted_iota(jnp.int32, (size, size), 0)
    col = lax.broadcasted_iota(jnp.int32, (size, size), 1)
    return jnp.where(col == source(row), 1.0, 0.0).astype(jnp.bfloat16)


def plan(owner, table, perm, slot, rank, count, load, moved_count, before, start):
    x, c = lax.axis_index("x"), lax.axis_index("c")
    for i in range(2 * SIDE):
        count[i] = 0
    for i in range(SIDE):
        load[i] = 0
    for i in range(SIDE * SIDE):
        moved_count[i] = 0
    for i in range(3 * CAP):
        table[SEND + i] = 0

    def number_tiles(q, carry):
        o = owner[q]
        h = o // 2
        slot[q] = count[o]
        rank[q] = load[h]
        count[o] = slot[q] + 1
        load[h] = rank[q] + 1
        return carry

    lax.fori_loop(0, TILES, number_tiles, 0)
    over = under = jnp.int32(0)
    ends = []
    for i in range(SIDE):
        before[i] = over
        start[i] = load[i] - under
        over = over + jnp.maximum(load[i] - CAP, 0)
        under = under + jnp.maximum(CAP - load[i], 0)
        ends.append(under)

    def place_tiles(q, most):
        o = owner[q]
        h = o // 2
        moves = rank[q] >= CAP
        number = before[h] + rank[q] - CAP
        there = sum((number >= end).astype(jnp.int32) for end in ends)
        target = jnp.where(moves, there, h)
        pos = jnp.where(moves, start[target] + number, rank[q])
        perm[target * CAP + pos] = q
        pair = h * SIDE + target
        order = moved_count[pair]
        moved_count[pair] = order + moves.astype(jnp.int32)
        place = jnp.where(o % 2 == c, slot[q], CAP + slot[q])
        shift = (target - h) & (SIDE - 1)

        @pl.when(jnp.logical_and(moves, h == x))
        def _():
            table[SEND + (shift - 1) * CAP + order] = place

        @pl.when(target == x)
        def _():
            arriving = 2 * CAP + (order // QUAD) * 3 * QUAD + (shift - 1) * QUAD + order % QUAD
            table[GATHER + pos] = jnp.where(moves, arriving, place)

        return jnp.maximum(most, jnp.where(moves, order, -1))

    most = lax.fori_loop(0, TILES, place_tiles, jnp.int32(-1))
    table[ROUNDS] = (most + QUAD) // QUAD


def amplitude_kernel(owner, amp, out, table, perm, *scratch):
    plan(owner, table, perm, *scratch)
    by_ky = one_hot(amp.shape[0], lambda i: ((i // 4) % 4) * 16 + (i // 16) * 4 + i % 4)

    def load(base):
        return jnp.dot(by_ky, amp[:, pl.ds(base, WINDOW)], preferred_element_type=jnp.float32)

    for g in range(TILES // QUAD):
        columns = four_tiles(load, [perm[QUAD * g + j] * TW for j in range(QUAD)], TILES * TW)
        x, at = g // (CAP // QUAD), (g % (CAP // QUAD)) * QUAD * TW
        for k, column in enumerate(columns):
            for ky in range(SIDE):
                out[x * SIDE + ky, :, at + k * LANES : at + (k + 1) * LANES] = column[
                    ky * 16 : (ky + 1) * 16
                ].astype(jnp.bfloat16)


def order_amplitudes(tile_owner, amplitudes):
    sm = lambda n: pltpu.SMEM((n,), jnp.int32)
    smem = pl.BlockSpec(memory_space=pltpu.SMEM)
    vmem = pl.BlockSpec(memory_space=pltpu.VMEM)
    return pl.pallas_call(
        amplitude_kernel,
        out_shape=(
            jax.ShapeDtypeStruct((SIDE * SIDE, 16, WIDTH), jnp.bfloat16),
            jax.ShapeDtypeStruct((LANES,), jnp.int32),
        ),
        in_specs=[smem, vmem],
        out_specs=(vmem, smem),
        scratch_shapes=[sm(TILES), sm(TILES), sm(TILES), sm(8), sm(4), sm(16), sm(4), sm(4)],
        compiler_params=VMEM,
        name="order_amplitudes",
    )(tile_owner, amplitudes)


def tile_rows(pool, table, first, out, at):
    def rows(i, carry):
        here = pl.ds(pl.multiple_of(i * 48, 16), 48)
        load = lambda base: pool[here, pl.ds(base, WINDOW)].astype(jnp.float32)
        starts = [table[first + j] * TW for j in range(QUAD)]
        for k, column in enumerate(four_tiles(load, starts, pool.shape[1])):
            out[here, at + k * LANES : at + (k + 1) * LANES] = column.astype(jnp.bfloat16)
        return carry

    lax.fori_loop(0, HALF // 48, rows, 0)


def fill_pool(sources, pool, sems):
    half = pl.ds(pl.multiple_of(lax.axis_index("c") * HALF, 16), HALF)
    copies = []
    at = 0
    for i, ref in enumerate(sources):
        src = ref.at[half] if i < 2 else ref
        width = ref.shape[1]
        copies.append(pltpu.make_async_copy(src, pool.at[:, pl.ds(at, width)], sems.at[i]))
        at += width
    for copy in copies:
        copy.start()
    for copy in copies:
        copy.wait()


def pack_kernel(number, table, mine, other, out1, out2, out3, pool, sems):
    fill_pool((mine, other), pool, sems)
    for s, out in enumerate((out1, out2, out3)):
        tile_rows(pool, table, SEND + s * CAP + number * QUAD, out, 0)


def assemble_kernel(n, table, *refs):
    sources, out, pool, sems = refs[: 2 + n], refs[2 + n], refs[3 + n], refs[4 + n]
    fill_pool(sources, pool, sems)
    for g in range(CAP // QUAD):
        tile_rows(pool, table, GATHER + g * QUAD, out, g * QUAD * TW)


def pack(number, table, mine, other):
    anywhere = pl.BlockSpec(memory_space=pl.ANY)
    return pl.pallas_call(
        functools.partial(pack_kernel, number),
        out_shape=tuple(jax.ShapeDtypeStruct((HALF, QUAD * TW), jnp.bfloat16) for _ in range(3)),
        in_specs=[pl.BlockSpec(memory_space=pltpu.SMEM), anywhere, anywhere],
        out_specs=tuple(pl.BlockSpec(memory_space=pltpu.VMEM) for _ in range(3)),
        scratch_shapes=[pltpu.VMEM((HALF, 2 * WIDTH), jnp.bfloat16), pltpu.SemaphoreType.DMA((2,))],
        compiler_params=VMEM,
        name="pack",
    )(table, mine, other)


def assemble(table, mine, other, received):
    anywhere = pl.BlockSpec(memory_space=pl.ANY)
    n = len(received)
    return pl.pallas_call(
        functools.partial(assemble_kernel, n),
        out_shape=jax.ShapeDtypeStruct((HALF, WIDTH), jnp.bfloat16),
        in_specs=[pl.BlockSpec(memory_space=pltpu.SMEM)] + [anywhere] * (2 + n),
        out_specs=pl.BlockSpec(memory_space=pltpu.VMEM),
        scratch_shapes=[
            pltpu.VMEM((HALF, 2 * WIDTH + n * QUAD * TW), jnp.bfloat16),
            pltpu.SemaphoreType.DMA((2 + n,)),
        ],
        compiler_params=VMEM,
        name="assemble",
    )(table, mine, other, *received)


def exchange(number, table, mine, other):
    return [ring(part, "x", s + 1) for s, part in enumerate(pack(number, table, mine, other))]


def balanced(table, mine, other):
    first = exchange(0, table, mine, other)

    def more(table, mine, other, *received):
        for number in range(1, CAP // QUAD):
            received = received + tuple(exchange(number, table, mine, other))
        return assemble(table, mine, other, received)

    def enough(table, mine, other, *received):
        return assemble(table, mine, other, received)

    return lax.cond(table[ROUNDS] > 1, more, enough, table, mine, other, *first)


def encode(value):
    lane = lax.broadcasted_iota(jnp.int32, value.shape, 1)
    top = jnp.max(jnp.where(lane < HALF, jnp.abs(value), 0.0), axis=1, keepdims=True)
    code = jnp.ceil(jnp.log2(jnp.maximum(top, 1e-33)) * STEPS)
    level = jnp.floor(value * (jnp.exp2(code * (-1.0 / STEPS)) * LEVELS) + 0.5)
    return jnp.where(lane < HALF, level, code).astype(jnp.int32).astype(jnp.int16)


def decode(coded):
    wide = coded.astype(jnp.int32).astype(jnp.float32)
    scale = jnp.exp2(wide[:, HALF : HALF + 1] * (1.0 / STEPS)) * (1.0 / LEVELS)
    return wide * scale


def product_kernel(kind, *refs):
    amps, blocks, rest = refs[:5], refs[5:15], refs[15:]
    n_in = {"far": 0, "next": 1, "prev": 1, "last": 2}[kind]
    incoming, outs = rest[:n_in], rest[n_in:-5]
    raw, ordered, held, amp_sems, block_sems = rest[-5:]
    amp_copies, at = [], 0
    for i, ref in enumerate(amps):
        amp_copies.append(pltpu.make_async_copy(ref, raw.at[pl.ds(at, ref.shape[0])], amp_sems.at[i]))
        at += ref.shape[0]
    block_copies, chunk, at = [], 0, 0
    for i, ref in enumerate(blocks):
        size = ref.shape[0]
        block_copies.append(
            (chunk, pltpu.make_async_copy(ref, held.at[chunk, pl.ds(at, size)], block_sems.at[i]))
        )
        at += size
        if at == HALF:
            chunk, at = chunk + 1, 0
    for copy in amp_copies:
        copy.start()
    for _, copy in block_copies:
        copy.start()
    for k in range(8):
        held[k, HALF:, :] = jnp.zeros((PADDED - HALF, WIDTH), jnp.bfloat16)
    for copy in amp_copies:
        copy.wait()
    by_kz = one_hot(4 * 64, lambda i: ((i // 16) % 4) * 64 + ((i // 4) % 4) * 16 + (i // 64) * 4 + i % 4)
    ordered[...] = jnp.dot(by_kz, raw[...], preferred_element_type=jnp.float32).astype(jnp.bfloat16)
    for k in range(8):
        for index, copy in block_copies:
            if index == k:
                copy.wait()
        for part in range(2):
            rows = slice(part * CUT, (part + 1) * CUT)
            value = lax.dot_general(
                ordered[rows, :], held[k], (((1,), (1,)), ((), ())), preferred_element_type=jnp.float32
            )
            if kind == "next" and part == 0 or kind == "prev" and part == 1:
                value = value + decode(incoming[0][k])
            if kind == "last":
                value = value + decode(incoming[0][k, rows]) + decode(incoming[1][k, rows])
            coded = encode(value)
            if kind == "far":
                outs[part][k] = coded
            elif kind == "last":
                outs[0][2 * part, k] = coded[:64]
                outs[0][2 * part + 1, k] = coded[64:]
            else:
                outs[0][k, rows] = coded


def product(kind, amps, blocks, incoming=()):
    shape = {"far": (8, CUT, PADDED), "last": (SIDE, 8, 64, PADDED)}.get(kind, (8, 2 * CUT, PADDED))
    anywhere = pl.BlockSpec(memory_space=pl.ANY)
    vmem = pl.BlockSpec(memory_space=pltpu.VMEM)
    out = jax.ShapeDtypeStruct(shape, jnp.int16)
    return pl.pallas_call(
        functools.partial(product_kernel, kind),
        out_shape=(out, out) if kind == "far" else (out,),
        in_specs=[anywhere] * 15 + [vmem] * len(incoming),
        out_specs=(vmem, vmem) if kind == "far" else (vmem,),
        scratch_shapes=[
            pltpu.VMEM((2 * CUT, WIDTH), jnp.bfloat16),
            pltpu.VMEM((2 * CUT, WIDTH), jnp.bfloat16),
            pltpu.VMEM((8, PADDED, WIDTH), jnp.bfloat16),
            pltpu.SemaphoreType.DMA((5,)),
            pltpu.SemaphoreType.DMA((10,)),
        ],
        compiler_params=VMEM,
        cost_estimate=pl.CostEstimate(flops=2 * 256 * WIDTH * 2048, bytes_accessed=10 << 20, transcendentals=0),
        name="product_" + kind,
    )(*amps, *blocks, *incoming)


def finish_kernel(got, virt, occ, out):
    y, c = lax.axis_index("y"), lax.axis_index("c")
    source = pl.program_id(0)
    for ya in range(SIDE):
        for h in range(2):
            k = ((ya - y) & (SIDE - 1)) * 2 + jnp.bitwise_xor(c, h)
            at = ya * 2 * HALF + h * HALF
            for zr in range(SIDE):
                first = pl.multiple_of(((zr - source) & (SIDE - 1)) * 16, 16)
                value = decode(got[0, k, pl.ds(first, 16), :])[:, :HALF]
                rows = slice(zr * 16, (zr + 1) * 16)
                out[rows, at : at + HALF] = value / (virt[:, at : at + HALF] - occ[rows, :])


def finish(got, virt, occ):
    return pl.pallas_call(
        finish_kernel,
        grid=(SIDE,),
        out_shape=jax.ShapeDtypeStruct((64, SIDE * WIDTH), jnp.float32),
        in_specs=[
            pl.BlockSpec((1, 8, 64, PADDED), lambda i: (i, 0, 0, 0)),
            pl.BlockSpec((1, WIDTH), lambda i: (0, i)),
            pl.BlockSpec((64, 1), lambda i: (0, 0)),
        ],
        out_specs=pl.BlockSpec((64, WIDTH), lambda i: (0, i)),
        compiler_params=VMEM,
        name="finish",
    )(got, virt, occ)


def ring_pieces(piece, axis, cut):
    low = ring(piece, axis, 1)
    high = ring(piece, axis, -1)
    return piece, high, ring(low[:cut], axis, 1), ring(high[cut:], axis, -1), low


def on_device(amplitudes, integrals, tile_ids, tile_owner, occ_pairs, occ_energy, vir_energy):
    z, y, x, c = (lax.axis_index(name) for name in ALL)
    occ_dev = amplitudes.shape[0]
    sub = occ_dev // (SIDE * SIDE)
    mine = integrals[0]
    other = swap(mine)
    taken, table = order_amplitudes(tile_owner, amplitudes)
    arrived = lax.all_to_all(taken, ("x", "y"), split_axis=0, concat_axis=0, tiled=True)
    arrived = arrived.reshape(SIDE, occ_dev, WIDTH)

    shard = balanced(table, mine, other)
    blocks = []
    for piece in ring_pieces(shard, "y", CUT):
        blocks.append((piece, swap(piece)))
    own, high, far0, far1, low = blocks
    blocks = [*own, *high, far0[0], far1[0], far0[1], far1[1], *low]

    def pairs_of(xo):
        return lax.dynamic_index_in_dim(arrived, xo % SIDE, axis=0, keepdims=False)

    far = ring_pieces(pairs_of(x + 2), "z", 32)
    rest = jnp.concatenate([pairs_of(x + 1), pairs_of(x + 3), pairs_of(x)], axis=1)
    rest = ring_pieces(rest, "z", 32)
    part = lambda i: [p[:, i * WIDTH : (i + 1) * WIDTH] for p in rest]

    up, down = product("far", far, blocks)
    up, down = ring(up, "x", 1), ring(down, "x", -1)
    (nxt,) = product("next", part(0), blocks, (up,))
    from_low = ring(nxt, "x", 1)
    (prv,) = product("prev", part(1), blocks, (down,))
    from_high = ring(prv, "x", -1)
    (total,) = product("last", part(2), blocks, (from_low, from_high))
    got = lax.all_to_all(total, "z", split_axis=0, concat_axis=0, tiled=True)

    grid = occ_pairs.reshape(SIDE * SIDE, 2 * SIDE, SIDE * SIDE, sub, 2)
    here = lax.dynamic_slice(grid, (0, 2 * x + c, SIDE * z + y, 0, 0), (SIDE * SIDE, 1, 1, sub, 2))
    occ_sum = jnp.sum(jnp.take(occ_energy, here.reshape(occ_dev, 2), axis=0), axis=1)
    per_row = NVIR // TW
    second = jnp.take(vir_energy.reshape(per_row, TW), tile_ids % per_row, axis=0)
    virt_sum = (jnp.take(vir_energy, tile_ids // per_row)[:, None] + second).reshape(1, TILES * TW)
    return finish(got, virt_sum, occ_sum[:, None])[None]


def solution(mesh):
    chips = Mesh(mesh.devices.reshape(SIDE, SIDE, SIDE, 2), ALL)
    placed = (P(ALL, None), P(("x", "c"), ("z", "y"), None), P(), P(), P(), P(), P())
    return jax.shard_map(
        on_device, mesh=chips, in_specs=placed, out_specs=P(("z", "y"), ("x", "c"), None), check_vma=False
    )
```

```python
import functools

import jax
import jax.numpy as jnp
from jax import lax
from jax.experimental import pallas as pl
from jax.experimental.pallas import tpu as pltpu
from jax.sharding import Mesh, PartitionSpec as P

TW = 96
NVIR = 2016
SIDE = 4
TILES = 80
CAP = 20
QUAD = 4
LANES = 128
WINDOW = 2 * LANES
HALF = 240
PADDED = 256
WIDTH = CAP * TW
CUT = 128
LEVELS = 32000.0
STEPS = 256.0
ALL = ("z", "y", "x", "c")
SEND = 0
GATHER = 3 * CAP
ROUNDS = GATHER + CAP
VMEM = pltpu.CompilerParams(vmem_limit_bytes=48 * 1024 * 1024)


def ring(value, axis, shift):
    return lax.ppermute(value, axis, [(i, (i + shift) % SIDE) for i in range(SIDE)])


def swap(value):
    return lax.ppermute(value, "c", [(0, 1), (1, 0)])


def four_tiles(load, starts, limit):
    parts = []
    for start, want in zip(starts, (0, 96, 64, 160)):
        base = jnp.minimum((start // LANES) * LANES, limit - WINDOW)
        window = load(pl.multiple_of(base, LANES))
        parts.append(pltpu.roll(window, (want - (start - base)) & (WINDOW - 1), 1))
    a, b, c, d = parts
    lane = lax.broadcasted_iota(jnp.int32, (a.shape[0], LANES), 1)
    return (
        jnp.where(lane < 96, a[:, :LANES], b[:, :LANES]),
        jnp.where(lane < 64, b[:, LANES:], c[:, :LANES]),
        jnp.where(lane < 32, c[:, LANES:], d[:, LANES:]),
    )


def one_hot(size, source):
    row = lax.broadcasted_iota(jnp.int32, (size, size), 0)
    col = lax.broadcasted_iota(jnp.int32, (size, size), 1)
    return jnp.where(col == source(row), 1.0, 0.0).astype(jnp.bfloat16)


def plan_kernel(owner, out):
    x, c = (lax.axis_index(name).astype(jnp.float32) for name in "xc")
    i = lax.broadcasted_iota(jnp.int32, (TILES, TILES), 0)
    j = lax.broadcasted_iota(jnp.int32, (TILES, TILES), 1)
    across = lambda mask, value=1.0: jnp.sum(jnp.where(mask, value, 0.0), axis=1, keepdims=True)
    down = lambda mask, value=1.0: jnp.sum(jnp.where(mask, value, 0.0), axis=0, keepdims=True)
    earlier = j < i
    owner_row = owner[...].astype(jnp.float32)
    owner_col = across(i == j, owner_row)
    home_row, home = jnp.floor(owner_row * 0.5), jnp.floor(owner_col * 0.5)
    slot = across((owner_row == owner_col) & earlier)
    rank = across((home_row == home) & earlier)
    moves = rank >= CAP
    over = under = jnp.zeros((1, 1), jnp.float32)
    number = rank - CAP
    ends, starts = [], []
    for k in range(SIDE):
        load = across(home_row == k)
        number = number + jnp.where(home == k, over, 0.0)
        starts.append(load - under)
        over = over + jnp.maximum(load - CAP, 0.0)
        under = under + jnp.maximum(CAP - load, 0.0)
        ends.append(under)
    target = jnp.where(moves, sum(jnp.where(number >= end, 1.0, 0.0) for end in ends), home)
    start = sum(jnp.where(target == k, starts[k], 0.0) for k in range(SIDE))
    pos = jnp.where(moves, start + number, rank)
    moving = jnp.where(moves, home * SIDE + target, -1.0)
    order = across((down(i == j, moving) == moving) & earlier)
    place = jnp.where(owner_col - 2.0 * home == c, slot, CAP + slot)
    shift = target - home
    shift = jnp.where(shift < 0.0, shift + SIDE, shift) - 1.0
    lane = lax.broadcasted_iota(jnp.int32, (TILES, LANES), 1).astype(jnp.float32)
    row = lax.broadcasted_iota(jnp.int32, (TILES, LANES), 0).astype(jnp.float32)
    perm = down(lane == target * CAP + pos, row)
    outgoing = jnp.where(moves & (home == x), SEND + shift * CAP + order, -1.0)
    group = jnp.floor(order * (1.0 / QUAD))
    arriving = 2 * CAP + group * 3 * QUAD + shift * QUAD + order - group * QUAD
    incoming = jnp.where(target == x, GATHER + pos, -1.0)
    table = down(lane == outgoing, place) + down(lane == incoming, jnp.where(moves, arriving, place))
    most = jnp.max(jnp.where(moves, order, -1.0), axis=0, keepdims=True)
    rounds = jnp.floor((most + QUAD) * (1.0 / QUAD))
    table = jnp.where(lane[:1] == ROUNDS, rounds, table)
    out[0:1, :] = perm.astype(jnp.int32)
    out[1:2, :] = table.astype(jnp.int32)


def make_plan(tile_owner):
    vmem = pl.BlockSpec(memory_space=pltpu.VMEM)
    return pl.pallas_call(
        plan_kernel,
        out_shape=jax.ShapeDtypeStruct((2, LANES), jnp.int32),
        in_specs=[vmem],
        out_specs=vmem,
        name="make_plan",
    )(tile_owner[None, :])


def amplitude_kernel(table, amp, after, *outs):
    x = lax.axis_index("x")
    load = lambda base: amp[:, pl.ds(base, WINDOW)].astype(jnp.float32)
    for s, out in enumerate(outs):
        first = ((x + s) % SIDE) * CAP
        for g in range(0, CAP, QUAD):
            starts = [table[0, first + g + j] * TW for j in range(QUAD)]
            for k, column in enumerate(four_tiles(load, starts, TILES * TW)):
                at = g * TW + k * LANES
                out[:, at : at + LANES] = column.astype(jnp.bfloat16)


def order_amplitudes(table, amplitudes, after):
    vmem = pl.BlockSpec(memory_space=pltpu.VMEM)
    return pl.pallas_call(
        amplitude_kernel,
        out_shape=tuple(jax.ShapeDtypeStruct((64, WIDTH), jnp.bfloat16) for _ in range(SIDE)),
        in_specs=[pl.BlockSpec(memory_space=pltpu.SMEM), vmem, pl.BlockSpec(memory_space=pl.ANY)],
        out_specs=tuple(vmem for _ in range(SIDE)),
        compiler_params=VMEM,
        name="order_amplitudes",
    )(table, amplitudes, after)


def tile_rows(pool, table, first, out, at):
    def rows(i, carry):
        here = pl.ds(pl.multiple_of(i * 48, 16), 48)
        load = lambda base: pool[here, pl.ds(base, WINDOW)].astype(jnp.float32)
        starts = [table[1, first + j] * TW for j in range(QUAD)]
        for k, column in enumerate(four_tiles(load, starts, pool.shape[1])):
            out[here, at + k * LANES : at + (k + 1) * LANES] = column.astype(jnp.bfloat16)
        return carry

    lax.fori_loop(0, HALF // 48, rows, 0)


def fill_pool(sources, pool, sems):
    half = pl.ds(pl.multiple_of(lax.axis_index("c") * HALF, 16), HALF)
    copies = []
    at = 0
    for i, ref in enumerate(sources):
        src = ref.at[half] if i < 2 else ref
        width = ref.shape[1]
        copies.append(pltpu.make_async_copy(src, pool.at[:, pl.ds(at, width)], sems.at[i]))
        at += width
    for copy in copies:
        copy.start()
    for copy in copies:
        copy.wait()


def pack_kernel(number, table, mine, other, after, out1, out2, out3, pool, sems):
    fill_pool((mine, other), pool, sems)
    for s, out in enumerate((out1, out2, out3)):
        tile_rows(pool, table, SEND + s * CAP + number * QUAD, out, 0)


def assemble_kernel(table, mine, other, in1, in2, in3, extra, out, pool, sems):
    fill_pool((mine, other, in1, in2, in3), pool, sems)
    at, width = 2 * WIDTH + 3 * QUAD * TW, QUAD * TW

    @pl.when(table[1, ROUNDS] > 1)
    def _():
        copies = [
            pltpu.make_async_copy(extra.at[i], pool.at[:, pl.ds(at + i * width, width)], sems.at[i])
            for i in range(extra.shape[0])
        ]
        for copy in copies:
            copy.start()
        for copy in copies:
            copy.wait()

    for g in range(CAP // QUAD):
        tile_rows(pool, table, GATHER + g * QUAD, out, g * QUAD * TW)


def pack(number, table, mine, other, after):
    anywhere = pl.BlockSpec(memory_space=pl.ANY)
    return pl.pallas_call(
        functools.partial(pack_kernel, number),
        out_shape=tuple(jax.ShapeDtypeStruct((HALF, QUAD * TW), jnp.bfloat16) for _ in range(3)),
        in_specs=[pl.BlockSpec(memory_space=pltpu.SMEM), anywhere, anywhere, anywhere],
        out_specs=tuple(pl.BlockSpec(memory_space=pltpu.VMEM) for _ in range(3)),
        scratch_shapes=[pltpu.VMEM((HALF, 2 * WIDTH), jnp.bfloat16), pltpu.SemaphoreType.DMA((2,))],
        compiler_params=VMEM,
        name="pack",
    )(table, mine, other, after)


def assemble(table, mine, other, received, extra):
    anywhere = pl.BlockSpec(memory_space=pl.ANY)
    n = len(received) + extra.shape[0]
    return pl.pallas_call(
        assemble_kernel,
        out_shape=jax.ShapeDtypeStruct((HALF, WIDTH), jnp.bfloat16),
        in_specs=[pl.BlockSpec(memory_space=pltpu.SMEM)] + [anywhere] * 6,
        out_specs=pl.BlockSpec(memory_space=pltpu.VMEM),
        scratch_shapes=[
            pltpu.VMEM((HALF, 2 * WIDTH + n * QUAD * TW), jnp.bfloat16),
            pltpu.SemaphoreType.DMA((2 + n,)),
        ],
        compiler_params=VMEM,
        cost_estimate=pl.CostEstimate(flops=0, bytes_accessed=10 << 20, transcendentals=0),
        name="assemble",
    )(table, mine, other, *received, extra)


def send(packed):
    return [ring(part, "x", s + 1) for s, part in enumerate(packed)]


def later_rounds(table, mine, other):
    def more(table, mine, other):
        parts = []
        for number in range(1, CAP // QUAD):
            parts += send(pack(number, table, mine, other, parts[-1] if parts else table))
        return jnp.stack(parts)

    def none(table, mine, other):
        return jnp.zeros((3 * (CAP // QUAD - 1), HALF, QUAD * TW), mine.dtype)

    return lax.cond(table[1, ROUNDS] > 1, more, none, table, mine, other)


def encode(value):
    top = jnp.max(jnp.abs(value), axis=1, keepdims=True)
    code = jnp.ceil(jnp.log2(jnp.maximum(top, 1e-33)) * STEPS)
    level = jnp.floor(value * (jnp.exp2(code * (-1.0 / STEPS)) * LEVELS) + 0.5)
    return level.astype(jnp.int32).astype(jnp.int16), code.astype(jnp.int32).astype(jnp.int16)


def decode(coded):
    wide = coded.astype(jnp.int32).astype(jnp.float32)
    lane = lax.broadcasted_iota(jnp.int32, wide.shape, 1)
    code = jnp.sum(jnp.where(lane == HALF, wide, 0.0), axis=1, keepdims=True)
    return wide[:, :HALF] * (jnp.exp2(code * (1.0 / STEPS)) * (1.0 / LEVELS))


def put(out, k, level, code):
    out[k, :, :HALF] = level
    out[k, :, HALF:] = jnp.broadcast_to(code, (64, PADDED - HALF))


def code_far_kernel(n, *refs):
    sums, (up, down) = refs[: 2 * n], refs[2 * n :]
    for k in range(n):
        put(up, k, *encode(sums[k][...]))
        put(down, k, *encode(sums[n + k][...]))


def code_near_kernel(n, *refs):
    sums, (up, down, nxt, prv) = refs[: 2 * n], refs[2 * n :]
    step = pl.program_id(0)

    def run(first, second, out, extra):
        for k in range(n):
            put(out, k, *encode(sums[first + k][...] + decode(extra[k])))
        for k in range(n):
            put(second[0], k, *encode(sums[second[1] + k][...]))

    pl.when(step < 2)(lambda: run(0, (prv, n), nxt, up))
    pl.when(step >= 2)(lambda: run(n, (nxt, 0), prv, down))


def code_last_kernel(n, *refs):
    sums, (low, high, out) = refs[:n], refs[n:]
    for k in range(n):
        level, code = encode(sums[k][...] + decode(low[k]) + decode(high[k]))
        code = jnp.broadcast_to(code, (64, PADDED - HALF))
        for row in range(SIDE):
            rows = slice(16 * row, 16 * (row + 1))
            out[row, k, :, :HALF] = level[rows]
            out[row, k, :, HALF:] = code[rows]


def code_far(sums):
    n = len(sums)
    out = jax.ShapeDtypeStruct((n, CUT, PADDED), jnp.int16)
    block = pl.BlockSpec((n, 64, PADDED), lambda i: (0, i, 0))
    rows = lambda shift: pl.BlockSpec((64, HALF), lambda i: (i + shift, 0))
    return pl.pallas_call(
        functools.partial(code_far_kernel, n),
        out_shape=(out, out),
        grid=(2,),
        in_specs=[rows(0)] * n + [rows(2)] * n,
        out_specs=(block, block),
        compiler_params=VMEM,
        name="code_far",
    )(*sums, *sums)


def code_near(sums_next, sums_prev, up, down):
    n = len(sums_next)
    out = jax.ShapeDtypeStruct((n, 2 * CUT, PADDED), jnp.int16)
    block = pl.BlockSpec((n, 64, PADDED), lambda i: (0, i, 0))
    half = lambda shift: pl.BlockSpec((n, 64, PADDED), lambda i: (0, jnp.clip(i - shift, 0, 1), 0))
    rows = pl.BlockSpec((64, HALF), lambda i: (i, 0))
    return pl.pallas_call(
        functools.partial(code_near_kernel, n),
        out_shape=(out, out),
        grid=(4,),
        in_specs=[rows] * (2 * n) + [half(0), half(2)],
        out_specs=(block, block),
        compiler_params=VMEM,
        name="code_near",
    )(*sums_next, *sums_prev, up, down)


def code_last(sums, low, high):
    n = len(sums)
    block = pl.BlockSpec((n, 64, PADDED), lambda i: (0, i, 0))
    return pl.pallas_call(
        functools.partial(code_last_kernel, n),
        out_shape=jax.ShapeDtypeStruct((SIDE * SIDE, n, 16, PADDED), jnp.int16),
        grid=(4,),
        in_specs=[pl.BlockSpec((64, HALF), lambda i: (i, 0))] * n + [block, block],
        out_specs=pl.BlockSpec((SIDE, n, 16, PADDED), lambda i: (i, 0, 0, 0)),
        compiler_params=VMEM,
        name="code_last",
    )(*sums, low, high)


def finish_kernel(groups, *refs):
    c = lax.axis_index("c")
    got, (virt, occ, out) = refs[: len(groups)], refs[len(groups) :]
    spots = {up: (ref, 2 * k) for ref, group in zip(got, groups) for k, up in enumerate(group)}
    by_zr = one_hot(64, lambda i: ((i // 4) % 4) * 16 + (i // 16) * 4 + i % 4).astype(jnp.float32)
    for ya in range(SIDE):
        for h in range(2):
            parts = []
            for ys in range(SIDE):
                ref, k = spots[(ya - ys) % SIDE]
                parts.append(decode(ref[ys, k + jnp.bitwise_xor(c, h)]))
            value = jnp.dot(by_zr, jnp.concatenate(parts, axis=0), precision=lax.Precision.HIGHEST)
            at = slice((2 * ya + h) * HALF, (2 * ya + h + 1) * HALF)
            out[:, at] = value / (virt[:, at] - occ[...])


def finish(groups, got, virt, occ):
    block = lambda n: pl.BlockSpec((SIDE, n, 16, PADDED), lambda i: (i, 0, 0, 0))
    return pl.pallas_call(
        functools.partial(finish_kernel, groups),
        grid=(SIDE,),
        out_shape=jax.ShapeDtypeStruct((64, SIDE * WIDTH), jnp.float32),
        in_specs=[block(2 * len(group)) for group in groups]
        + [
            pl.BlockSpec((1, WIDTH), lambda i: (0, i)),
            pl.BlockSpec((64, 1), lambda i: (0, 0)),
        ],
        out_specs=pl.BlockSpec((64, WIDTH), lambda i: (0, i)),
        compiler_params=VMEM,
        name="finish",
    )(*got, virt, occ)


def ring_pieces(first, second):
    both = (first, second)
    steps = [ring(piece, axis, shift) for piece, axis, _ in both for shift in (1, -1)]
    steps = lax.optimization_barrier(tuple(steps))
    lows, highs = steps[0::2], steps[1::2]
    fars = []
    for (_, axis, cut), low, high in zip(both, lows, highs):
        fars += [ring(low[:cut], axis, 1), ring(high[cut:], axis, -1)]
    fars = lax.optimization_barrier(tuple(fars))
    return [
        (piece, high, *fars[2 * i : 2 * i + 2], low)
        for i, ((piece, _, _), low, high) in enumerate(zip(both, lows, highs))
    ]


def on_device(amplitudes, integrals, tile_ids, tile_owner, occ_pairs, occ_energy, vir_energy):
    z, y, x, c = (lax.axis_index(name) for name in ALL)
    occ_dev = amplitudes.shape[0]
    sub = occ_dev // (SIDE * SIDE)
    mine = integrals[0]
    other = swap(mine)
    table = make_plan(tile_owner)
    extra = later_rounds(table, mine, other)
    packed = pack(0, table, mine, other, extra)
    first = send(packed)
    last, *leaving = order_amplitudes(table, amplitudes, packed[0])
    prev, far, nxt = send(leaving)
    shard = assemble(table, mine, other, first, extra)
    arrived = jnp.concatenate([far, nxt, prev, last], axis=0)
    arrived, _ = lax.optimization_barrier((arrived, shard))
    shares, pieces = ring_pieces((shard, "y", CUT), (arrived, "z", 2 * occ_dev))
    own, high, far0, far1, low = [(piece, swap(piece)) for piece in shares]
    both = tuple(jnp.concatenate([far0[i], far1[i]], axis=0) for i in range(2))
    blocks = [own, high, both, low]
    by_k = one_hot(256, lambda i: (((i // 4) % 4 - z) % 4) * 64 + (i // 16) * 4 + i % 4)

    def pairs_of(number):
        own, high, far0, far1, low = pieces
        at = lambda p, n: p[n * occ_dev : (n + 1) * occ_dev]
        far = at(far0, number) if number < 2 else at(far1, number - 2)
        whole = jnp.concatenate([at(own, number), at(high, number), far, at(low, number)], axis=0)
        return jnp.dot(by_k, whole, preferred_element_type=jnp.float32).astype(whole.dtype)

    def product(a, b):
        return lax.dot_general(a, b, (((1,), (1,)), ((), ())), preferred_element_type=jnp.float32)

    def sums(number, blocks):
        return [product(pairs[number], b) for b in blocks]

    pairs = [pairs_of(number) for number in range(SIDE)]

    def reduced(blocks):
        up, down = code_far(sums(0, blocks))
        pairs[1], pairs[2], pairs[3], *_ = lax.optimization_barrier((*pairs[1:], up, down))

        def near(next_pairs, prev_pairs, *blocks):
            return [product(p, b) for p in (next_pairs, prev_pairs) for b in blocks]

        def nothing(*_):
            return [jnp.zeros((4 * occ_dev, HALF), jnp.float32) for _ in range(2 * len(blocks))]

        both = lax.cond(table[1, ROUNDS] >= 0, near, nothing, pairs[1], pairs[2], *blocks)
        n = len(blocks)
        nxt, prv = code_near(both[:n], both[n:], ring(up, "x", 1), ring(down, "x", -1))
        total = code_last(sums(3, blocks), ring(nxt, "x", 1), ring(prv, "x", -1))
        got = lax.all_to_all(total, ("z", "y"), split_axis=0, concat_axis=0, tiled=True)
        return got, up

    groups = ((0, 1, 2, 3),)
    got, sent = zip(*(reduced([half for up in group for half in blocks[up]]) for group in groups))
    occ_pairs, occ_energy, vir_energy, _ = lax.optimization_barrier(
        (occ_pairs, occ_energy, vir_energy, sent[0])
    )

    grid = occ_pairs.reshape(SIDE * SIDE, 2 * SIDE, SIDE * SIDE, sub, 2)
    here = lax.dynamic_slice(grid, (0, 2 * x + c, SIDE * z + y, 0, 0), (SIDE * SIDE, 1, 1, sub, 2))
    occ_sum = jnp.sum(jnp.take(occ_energy, here.reshape(occ_dev, 2), axis=0), axis=1)
    per_row = NVIR // TW
    second = jnp.take(vir_energy.reshape(per_row, TW), tile_ids % per_row, axis=0)
    virt_sum = (jnp.take(vir_energy, tile_ids // per_row)[:, None] + second).reshape(1, TILES * TW)
    return finish(groups, got, virt_sum, occ_sum[:, None])[None]


def solution(mesh):
    chips = Mesh(mesh.devices.reshape(SIDE, SIDE, SIDE, 2), ALL)
    placed = (P(ALL, None), P(("x", "c"), ("z", "y"), None), P(), P(), P(), P(), P())
    return jax.shard_map(
        on_device, mesh=chips, in_specs=placed, out_specs=P(("z", "y"), ("x", "c"), None), check_vma=False
    )
```

```python
import functools

import jax
import jax.numpy as jnp
from jax import lax
from jax.experimental import pallas as pl
from jax.experimental.pallas import tpu as pltpu
from jax.sharding import Mesh, PartitionSpec as P

TW = 96
NVIR = 2016
SIDE = 4
TILES = 80
CAP = 20
QUAD = 4
LANES = 128
WINDOW = 2 * LANES
HALF = 240
PADDED = 256
WIDTH = CAP * TW
CUT = 128
LEVELS = 32000.0
STEPS = 256.0
ALL = ("z", "y", "x", "c")
SEND = 0
GATHER = 3 * CAP
ROUNDS = GATHER + CAP
VMEM = pltpu.CompilerParams(vmem_limit_bytes=48 * 1024 * 1024)


def ring(value, axis, shift):
    return lax.ppermute(value, axis, [(i, (i + shift) % SIDE) for i in range(SIDE)])


def part_ring(up, down, axis):
    value = up if up is down else jnp.where(lax.axis_index("c") == 0, up, down)
    pairs = [(2 * i + c, 2 * ((i + 1 - 2 * c) % SIDE) + c) for i in range(SIDE) for c in range(2)]
    return lax.ppermute(value, (axis, "c"), pairs)


def swap(value):
    return lax.ppermute(value, "c", [(0, 1), (1, 0)])


def four_tiles(load, starts, limit):
    parts = []
    for start, want in zip(starts, (0, 96, 64, 160)):
        base = jnp.minimum((start // LANES) * LANES, limit - WINDOW)
        window = load(pl.multiple_of(base, LANES))
        parts.append(pltpu.roll(window, (want - (start - base)) & (WINDOW - 1), 1))
    a, b, c, d = parts
    lane = lax.broadcasted_iota(jnp.int32, (a.shape[0], LANES), 1)
    return (
        jnp.where(lane < 96, a[:, :LANES], b[:, :LANES]),
        jnp.where(lane < 64, b[:, LANES:], c[:, :LANES]),
        jnp.where(lane < 32, c[:, LANES:], d[:, LANES:]),
    )


def one_hot(size, source):
    row = lax.broadcasted_iota(jnp.int32, (size, size), 0)
    col = lax.broadcasted_iota(jnp.int32, (size, size), 1)
    return jnp.where(col == source(row), 1.0, 0.0).astype(jnp.bfloat16)


def plan_kernel(owner, out):
    x, c = (lax.axis_index(name).astype(jnp.float32) for name in "xc")
    i = lax.broadcasted_iota(jnp.int32, (TILES, TILES), 0)
    j = lax.broadcasted_iota(jnp.int32, (TILES, TILES), 1)
    across = lambda mask, value=1.0: jnp.sum(jnp.where(mask, value, 0.0), axis=1, keepdims=True)
    down = lambda mask, value=1.0: jnp.sum(jnp.where(mask, value, 0.0), axis=0, keepdims=True)
    earlier = j < i
    owner_row = owner[...].astype(jnp.float32)
    owner_col = across(i == j, owner_row)
    home_row, home = jnp.floor(owner_row * 0.5), jnp.floor(owner_col * 0.5)
    slot = across((owner_row == owner_col) & earlier)
    rank = across((home_row == home) & earlier)
    moves = rank >= CAP
    over = under = jnp.zeros((1, 1), jnp.float32)
    number = rank - CAP
    ends, starts = [], []
    for k in range(SIDE):
        load = across(home_row == k)
        number = number + jnp.where(home == k, over, 0.0)
        starts.append(load - under)
        over = over + jnp.maximum(load - CAP, 0.0)
        under = under + jnp.maximum(CAP - load, 0.0)
        ends.append(under)
    target = jnp.where(moves, sum(jnp.where(number >= end, 1.0, 0.0) for end in ends), home)
    start = sum(jnp.where(target == k, starts[k], 0.0) for k in range(SIDE))
    pos = jnp.where(moves, start + number, rank)
    moving = jnp.where(moves, home * SIDE + target, -1.0)
    order = across((down(i == j, moving) == moving) & earlier)
    place = jnp.where(owner_col - 2.0 * home == c, slot, CAP + slot)
    shift = target - home
    shift = jnp.where(shift < 0.0, shift + SIDE, shift) - 1.0
    lane = lax.broadcasted_iota(jnp.int32, (TILES, LANES), 1).astype(jnp.float32)
    row = lax.broadcasted_iota(jnp.int32, (TILES, LANES), 0).astype(jnp.float32)
    perm = down(lane == target * CAP + pos, row)
    outgoing = jnp.where(moves & (home == x), SEND + shift * CAP + order, -1.0)
    group = jnp.floor(order * (1.0 / QUAD))
    arriving = 2 * CAP + group * 3 * QUAD + shift * QUAD + order - group * QUAD
    incoming = jnp.where(target == x, GATHER + pos, -1.0)
    table = down(lane == outgoing, place) + down(lane == incoming, jnp.where(moves, arriving, place))
    most = jnp.max(jnp.where(moves, order, -1.0), axis=0, keepdims=True)
    rounds = jnp.floor((most + QUAD) * (1.0 / QUAD))
    table = jnp.where(lane[:1] == ROUNDS, rounds, table)
    out[0:1, :] = perm.astype(jnp.int32)
    out[1:2, :] = table.astype(jnp.int32)


def make_plan(tile_owner):
    vmem = pl.BlockSpec(memory_space=pltpu.VMEM)
    return pl.pallas_call(
        plan_kernel,
        out_shape=jax.ShapeDtypeStruct((2, LANES), jnp.int32),
        in_specs=[vmem],
        out_specs=vmem,
        name="make_plan",
    )(tile_owner[None, :])


def amplitude_kernel(table, amp, after, *outs):
    x = lax.axis_index("x")
    load = lambda base: amp[:, pl.ds(base, WINDOW)].astype(jnp.float32)
    for s, out in enumerate(outs):
        first = ((x + s) % SIDE) * CAP
        for g in range(0, CAP, QUAD):
            starts = [table[0, first + g + j] * TW for j in range(QUAD)]
            for k, column in enumerate(four_tiles(load, starts, TILES * TW)):
                at = g * TW + k * LANES
                out[:, at : at + LANES] = column.astype(jnp.bfloat16)


def order_amplitudes(table, amplitudes, after):
    vmem = pl.BlockSpec(memory_space=pltpu.VMEM)
    return pl.pallas_call(
        amplitude_kernel,
        out_shape=tuple(jax.ShapeDtypeStruct((64, WIDTH), jnp.bfloat16) for _ in range(SIDE)),
        in_specs=[pl.BlockSpec(memory_space=pltpu.SMEM), vmem, pl.BlockSpec(memory_space=pl.ANY)],
        out_specs=tuple(vmem for _ in range(SIDE)),
        compiler_params=VMEM,
        name="order_amplitudes",
    )(table, amplitudes, after)


def tile_rows(pool, table, first, out, at):
    def rows(i, carry):
        here = pl.ds(pl.multiple_of(i * 48, 16), 48)
        load = lambda base: pool[here, pl.ds(base, WINDOW)].astype(jnp.float32)
        starts = [table[1, first + j] * TW for j in range(QUAD)]
        for k, column in enumerate(four_tiles(load, starts, pool.shape[1])):
            out[here, at + k * LANES : at + (k + 1) * LANES] = column.astype(jnp.bfloat16)
        return carry

    lax.fori_loop(0, HALF // 48, rows, 0)


def fill_pool(sources, pool, sems):
    half = pl.ds(pl.multiple_of(lax.axis_index("c") * HALF, 16), HALF)
    copies = []
    at = 0
    for i, ref in enumerate(sources):
        src = ref.at[half] if i < 2 else ref
        width = ref.shape[1]
        copies.append(pltpu.make_async_copy(src, pool.at[:, pl.ds(at, width)], sems.at[i]))
        at += width
    for copy in copies:
        copy.start()
    for copy in copies:
        copy.wait()


def pack_kernel(number, table, mine, other, after, out1, out2, out3, pool, sems):
    fill_pool((mine, other), pool, sems)
    for s, out in enumerate((out1, out2, out3)):
        tile_rows(pool, table, SEND + s * CAP + number * QUAD, out, 0)


def assemble_kernel(table, mine, other, in1, in2, in3, extra, out, pool, sems):
    fill_pool((mine, other, in1, in2, in3), pool, sems)
    at, width = 2 * WIDTH + 3 * QUAD * TW, QUAD * TW

    @pl.when(table[1, ROUNDS] > 1)
    def _():
        copies = [
            pltpu.make_async_copy(extra.at[i], pool.at[:, pl.ds(at + i * width, width)], sems.at[i])
            for i in range(extra.shape[0])
        ]
        for copy in copies:
            copy.start()
        for copy in copies:
            copy.wait()

    for g in range(CAP // QUAD):
        tile_rows(pool, table, GATHER + g * QUAD, out, g * QUAD * TW)


def pack(number, table, mine, other, after):
    anywhere = pl.BlockSpec(memory_space=pl.ANY)
    return pl.pallas_call(
        functools.partial(pack_kernel, number),
        out_shape=tuple(jax.ShapeDtypeStruct((HALF, QUAD * TW), jnp.bfloat16) for _ in range(3)),
        in_specs=[pl.BlockSpec(memory_space=pltpu.SMEM), anywhere, anywhere, anywhere],
        out_specs=tuple(pl.BlockSpec(memory_space=pltpu.VMEM) for _ in range(3)),
        scratch_shapes=[pltpu.VMEM((HALF, 2 * WIDTH), jnp.bfloat16), pltpu.SemaphoreType.DMA((2,))],
        compiler_params=VMEM,
        name="pack",
    )(table, mine, other, after)


def assemble(table, mine, other, received, extra):
    anywhere = pl.BlockSpec(memory_space=pl.ANY)
    n = len(received) + extra.shape[0]
    return pl.pallas_call(
        assemble_kernel,
        out_shape=jax.ShapeDtypeStruct((HALF, WIDTH), jnp.bfloat16),
        in_specs=[pl.BlockSpec(memory_space=pltpu.SMEM)] + [anywhere] * 6,
        out_specs=pl.BlockSpec(memory_space=pltpu.VMEM),
        scratch_shapes=[
            pltpu.VMEM((HALF, 2 * WIDTH + n * QUAD * TW), jnp.bfloat16),
            pltpu.SemaphoreType.DMA((2 + n,)),
        ],
        compiler_params=VMEM,
        cost_estimate=pl.CostEstimate(flops=0, bytes_accessed=10 << 20, transcendentals=0),
        name="assemble",
    )(table, mine, other, *received, extra)


def send(packed):
    return [ring(part, "x", s + 1) for s, part in enumerate(packed)]


def later_rounds(table, mine, other):
    def more(table, mine, other):
        parts = []
        for number in range(1, CAP // QUAD):
            parts += send(pack(number, table, mine, other, parts[-1] if parts else table))
        return jnp.stack(parts)

    def none(table, mine, other):
        return jnp.zeros((3 * (CAP // QUAD - 1), HALF, QUAD * TW), mine.dtype)

    return lax.cond(table[1, ROUNDS] > 1, more, none, table, mine, other)


def encode(value):
    top = jnp.max(jnp.abs(value), axis=1, keepdims=True)
    code = jnp.ceil(jnp.log2(jnp.maximum(top, 1e-33)) * STEPS)
    level = jnp.floor(value * (jnp.exp2(code * (-1.0 / STEPS)) * LEVELS) + 0.5)
    return level.astype(jnp.int32).astype(jnp.int16), code.astype(jnp.int32).astype(jnp.int16)


def decode(coded):
    wide = coded.astype(jnp.int32).astype(jnp.float32)
    lane = lax.broadcasted_iota(jnp.int32, wide.shape, 1)
    code = jnp.sum(jnp.where(lane == HALF, wide, 0.0), axis=1, keepdims=True)
    return wide[:, :HALF] * (jnp.exp2(code * (1.0 / STEPS)) * (1.0 / LEVELS))


def put(out, k, level, code):
    out[k, :, :HALF] = level
    out[k, :, HALF:] = jnp.broadcast_to(code, (64, PADDED - HALF))


def code_far_kernel(n, *refs):
    for k in range(n):
        put(refs[n], k, *encode(refs[k][...]))


def code_near_kernel(n, *refs):
    sums, (arrived, nxt, prv) = refs[: 2 * n], refs[2 * n :]
    c = lax.axis_index("c")

    def run(first, out, other_first, other_out):
        for k in range(n):
            put(out, k, *encode(sums[first + k][...] + decode(arrived[k])))
        for k in range(n):
            put(other_out, k, *encode(sums[other_first + k][...]))

    pl.when(c == 0)(lambda: run(0, nxt, n, prv))
    pl.when(c != 0)(lambda: run(n, prv, 0, nxt))


def code_last_kernel(n, *refs):
    sums, (low, high, out) = refs[:n], refs[n:]
    for k in range(n):
        level, code = encode(sums[k][...] + decode(low[k]) + decode(high[k]))
        code = jnp.broadcast_to(code, (64, PADDED - HALF))
        for row in range(SIDE):
            rows = slice(16 * row, 16 * (row + 1))
            out[row, k, :, :HALF] = level[rows]
            out[row, k, :, HALF:] = code[rows]


def code_far(sums):
    n = len(sums)
    return pl.pallas_call(
        functools.partial(code_far_kernel, n),
        out_shape=jax.ShapeDtypeStruct((n, 2 * CUT, PADDED), jnp.int16),
        grid=(4,),
        in_specs=[pl.BlockSpec((64, HALF), lambda i: (i, 0))] * n,
        out_specs=pl.BlockSpec((n, 64, PADDED), lambda i: (0, i, 0)),
        compiler_params=VMEM,
        name="code_far",
    )(*sums)


def code_near(sums_next, sums_prev, arrived):
    n = len(sums_next)
    out = jax.ShapeDtypeStruct((n, 2 * CUT, PADDED), jnp.int16)
    block = pl.BlockSpec((n, 64, PADDED), lambda i: (0, i, 0))
    return pl.pallas_call(
        functools.partial(code_near_kernel, n),
        out_shape=(out, out),
        grid=(4,),
        in_specs=[pl.BlockSpec((64, HALF), lambda i: (i, 0))] * (2 * n) + [block],
        out_specs=(block, block),
        compiler_params=VMEM,
        name="code_near",
    )(*sums_next, *sums_prev, arrived)


def code_last(sums, low, high):
    n = len(sums)
    block = pl.BlockSpec((n, 64, PADDED), lambda i: (0, i, 0))
    return pl.pallas_call(
        functools.partial(code_last_kernel, n),
        out_shape=jax.ShapeDtypeStruct((SIDE * SIDE, n, 16, PADDED), jnp.int16),
        grid=(4,),
        in_specs=[pl.BlockSpec((64, HALF), lambda i: (i, 0))] * n + [block, block],
        out_specs=pl.BlockSpec((SIDE, n, 16, PADDED), lambda i: (i, 0, 0, 0)),
        compiler_params=VMEM,
        name="code_last",
    )(*sums, low, high)


def finish_kernel(groups, *refs):
    c = lax.axis_index("c")
    got, (virt, occ, out) = refs[: len(groups)], refs[len(groups) :]
    spots = {up: (ref, 2 * k) for ref, group in zip(got, groups) for k, up in enumerate(group)}
    by_zr = one_hot(64, lambda i: ((i // 4) % 4) * 16 + (i // 16) * 4 + i % 4).astype(jnp.float32)
    for ya in range(SIDE):
        for h in range(2):
            parts = []
            for ys in range(SIDE):
                ref, k = spots[(ya - ys) % SIDE]
                parts.append(ref[ys, k + jnp.bitwise_xor(c, h)])
            value = decode(jnp.concatenate(parts, axis=0))
            value = jnp.dot(by_zr, value, precision=lax.Precision.HIGHEST)
            j = 2 * ya + h
            out[:, j * HALF : (j + 1) * HALF] = value / (virt[j : j + 1, :HALF] - occ[...])


def finish(groups, got, virt, occ):
    block = lambda n: pl.BlockSpec((SIDE, n, 16, PADDED), lambda i: (i, 0, 0, 0))
    return pl.pallas_call(
        functools.partial(finish_kernel, groups),
        grid=(SIDE,),
        out_shape=jax.ShapeDtypeStruct((64, SIDE * WIDTH), jnp.float32),
        in_specs=[block(2 * len(group)) for group in groups]
        + [
            pl.BlockSpec((8, PADDED), lambda i: (i, 0)),
            pl.BlockSpec((64, 1), lambda i: (0, 0)),
        ],
        out_specs=pl.BlockSpec((64, WIDTH), lambda i: (0, i)),
        compiler_params=VMEM,
        name="finish",
    )(*got, virt, occ)


def ring_pieces(first, second):
    both = (first, second)
    steps = [ring(piece, axis, shift) for piece, axis, _ in both for shift in (1, -1)]
    steps = lax.optimization_barrier(tuple(steps))
    lows, highs = steps[0::2], steps[1::2]
    fars = []
    for (_, axis, cut), low, high in zip(both, lows, highs):
        fars += [ring(low[:cut], axis, 1), ring(high[cut:], axis, -1)]
    fars = lax.optimization_barrier(tuple(fars))
    return [
        (piece, high, *fars[2 * i : 2 * i + 2], low)
        for i, ((piece, _, _), low, high) in enumerate(zip(both, lows, highs))
    ]


def on_device(amplitudes, integrals, tile_ids, tile_owner, occ_pairs, occ_energy, vir_energy):
    z, y, x, c = (lax.axis_index(name) for name in ALL)
    occ_dev = amplitudes.shape[0]
    sub = occ_dev // (SIDE * SIDE)
    mine = integrals[0]
    other = swap(mine)
    table = make_plan(tile_owner)
    extra = later_rounds(table, mine, other)
    packed = pack(0, table, mine, other, extra)
    first = send(packed)
    last, *leaving = order_amplitudes(table, amplitudes, packed[0])
    prev, far, nxt = send(leaving)
    shard = assemble(table, mine, other, first, extra)
    arrived = jnp.concatenate([far, nxt, prev, last], axis=0)
    arrived, _ = lax.optimization_barrier((arrived, shard))
    shares, pieces = ring_pieces((shard, "y", CUT), (arrived, "z", 2 * occ_dev))
    own, high, far0, far1, low = [(piece, swap(piece)) for piece in shares]
    both = tuple(jnp.concatenate([far0[i], far1[i]], axis=0) for i in range(2))
    blocks = [own, high, both, low]
    by_k = one_hot(256, lambda i: (((i // 4) % 4 - z) % 4) * 64 + (i // 16) * 4 + i % 4)

    def pairs_of(number):
        own, high, far0, far1, low = pieces
        at = lambda p, n: p[n * occ_dev : (n + 1) * occ_dev]
        far = at(far0, number) if number < 2 else at(far1, number - 2)
        whole = jnp.concatenate([at(own, number), at(high, number), far, at(low, number)], axis=0)
        return jnp.dot(by_k, whole, preferred_element_type=jnp.float32).astype(whole.dtype)

    def product(a, b):
        return lax.dot_general(a, b, (((1,), (1,)), ((), ())), preferred_element_type=jnp.float32)

    def sums(number, blocks):
        return [product(pairs[number], b) for b in blocks]

    pairs = [pairs_of(number) for number in range(SIDE)]

    def near_sums(next_pairs, prev_pairs, *blocks):
        return [product(p, b) for p in (next_pairs, prev_pairs) for b in blocks]

    def no_sums(next_pairs, prev_pairs, *blocks):
        return [jnp.zeros((4 * occ_dev, HALF), jnp.float32) for _ in range(2 * len(blocks))]

    groups = ((0, 1), (2, 3))
    parts = [[half for up in group for half in blocks[up]] for group in groups]
    sent = [code_far(sums(0, part)) for part in parts]
    pairs[1], pairs[2], pairs[3], *_ = lax.optimization_barrier((*pairs[1:], *sent))
    far_sums = [part_ring(value, value, "x") for value in sent]
    leaving, behind = [], pairs[1:3]
    for part, arriving in zip(parts, far_sums):
        both = lax.cond(table[1, ROUNDS] >= 0, near_sums, no_sums, *behind, *part)
        leaving.append(code_near(both[: len(part)], both[len(part) :], arriving))
        *behind, _, _ = lax.optimization_barrier((pairs[1], pairs[2], *leaving[-1]))
    near_arrived = [(ring(nxt, "x", 1), ring(prv, "x", -1)) for nxt, prv in leaving]
    pairs[3], *_ = lax.optimization_barrier((pairs[3], *leaving[-1]))
    last_sums = [sums(3, part) for part in parts]
    got = []
    for sums_, arriving in zip(last_sums, near_arrived):
        total = code_last(sums_, *arriving)
        got.append(lax.all_to_all(total, ("z", "y"), split_axis=0, concat_axis=0, tiled=True))
    sent = leaving[-1]
    occ_pairs, occ_energy, vir_energy, _ = lax.optimization_barrier(
        (occ_pairs, occ_energy, vir_energy, sent[0])
    )

    grid = occ_pairs.reshape(SIDE * SIDE, 2 * SIDE, SIDE * SIDE, sub, 2)
    here = lax.dynamic_slice(grid, (0, 2 * x + c, SIDE * z + y, 0, 0), (SIDE * SIDE, 1, 1, sub, 2))
    occ_sum = jnp.sum(jnp.take(occ_energy, here.reshape(occ_dev, 2), axis=0), axis=1)
    per_row = NVIR // TW
    second = jnp.take(vir_energy.reshape(per_row, TW), tile_ids % per_row, axis=0)
    virt_sum = (jnp.take(vir_energy, tile_ids // per_row)[:, None] + second).reshape(8 * SIDE, HALF)
    virt_sum = jnp.pad(virt_sum, ((0, 0), (0, PADDED - HALF)))
    return finish(groups, got, virt_sum, occ_sum[:, None])[None]


def solution(mesh):
    chips = Mesh(mesh.devices.reshape(SIDE, SIDE, SIDE, 2), ALL)
    placed = (P(ALL, None), P(("x", "c"), ("z", "y"), None), P(), P(), P(), P(), P())
    return jax.shard_map(
        on_device, mesh=chips, in_specs=placed, out_specs=P(("z", "y"), ("x", "c"), None), check_vma=False
    )
```

```python
import functools

import jax
import jax.numpy as jnp
from jax import lax
from jax.experimental import pallas as pl
from jax.experimental.pallas import tpu as pltpu
from jax.sharding import Mesh, PartitionSpec as P

TW = 96
NVIR = 2016
SIDE = 4
TILES = 80
CAP = 20
QUAD = 4
LANES = 128
WINDOW = 2 * LANES
HALF = 240
PADDED = 256
WIDTH = CAP * TW
CUT = 128
LEVELS = 32000.0
STEPS = 256.0
ALL = ("z", "y", "x", "c")
SEND = 0
GATHER = 3 * CAP
ROUNDS = GATHER + CAP
VMEM = pltpu.CompilerParams(vmem_limit_bytes=48 * 1024 * 1024)


def ring(value, axis, shift):
    return lax.ppermute(value, axis, [(i, (i + shift) % SIDE) for i in range(SIDE)])


def part_ring(up, down, axis):
    value = up if up is down else jnp.where(lax.axis_index("c") == 0, up, down)
    pairs = [(2 * i + c, 2 * ((i + 1 - 2 * c) % SIDE) + c) for i in range(SIDE) for c in range(2)]
    return lax.ppermute(value, (axis, "c"), pairs)


def swap(value):
    return lax.ppermute(value, "c", [(0, 1), (1, 0)])


def four_tiles(load, starts, limit):
    parts = []
    for start, want in zip(starts, (0, 96, 64, 160)):
        base = jnp.minimum((start // LANES) * LANES, limit - WINDOW)
        window = load(pl.multiple_of(base, LANES))
        parts.append(pltpu.roll(window, (want - (start - base)) & (WINDOW - 1), 1))
    a, b, c, d = parts
    lane = lax.broadcasted_iota(jnp.int32, (a.shape[0], LANES), 1)
    return (
        jnp.where(lane < 96, a[:, :LANES], b[:, :LANES]),
        jnp.where(lane < 64, b[:, LANES:], c[:, :LANES]),
        jnp.where(lane < 32, c[:, LANES:], d[:, LANES:]),
    )


def one_hot(size, source):
    row = lax.broadcasted_iota(jnp.int32, (size, size), 0)
    col = lax.broadcasted_iota(jnp.int32, (size, size), 1)
    return jnp.where(col == source(row), 1.0, 0.0).astype(jnp.bfloat16)


def plan_kernel(owner, out):
    x, c = (lax.axis_index(name).astype(jnp.float32) for name in "xc")
    i = lax.broadcasted_iota(jnp.int32, (TILES, TILES), 0)
    j = lax.broadcasted_iota(jnp.int32, (TILES, TILES), 1)
    across = lambda mask, value=1.0: jnp.sum(jnp.where(mask, value, 0.0), axis=1, keepdims=True)
    down = lambda mask, value=1.0: jnp.sum(jnp.where(mask, value, 0.0), axis=0, keepdims=True)
    earlier = j < i
    owner_row = owner[...].astype(jnp.float32)
    owner_col = across(i == j, owner_row)
    home_row, home = jnp.floor(owner_row * 0.5), jnp.floor(owner_col * 0.5)
    slot = across((owner_row == owner_col) & earlier)
    rank = across((home_row == home) & earlier)
    moves = rank >= CAP
    over = under = jnp.zeros((1, 1), jnp.float32)
    number = rank - CAP
    ends, starts = [], []
    for k in range(SIDE):
        load = across(home_row == k)
        number = number + jnp.where(home == k, over, 0.0)
        starts.append(load - under)
        over = over + jnp.maximum(load - CAP, 0.0)
        under = under + jnp.maximum(CAP - load, 0.0)
        ends.append(under)
    target = jnp.where(moves, sum(jnp.where(number >= end, 1.0, 0.0) for end in ends), home)
    start = sum(jnp.where(target == k, starts[k], 0.0) for k in range(SIDE))
    pos = jnp.where(moves, start + number, rank)
    moving = jnp.where(moves, home * SIDE + target, -1.0)
    order = across((down(i == j, moving) == moving) & earlier)
    place = jnp.where(owner_col - 2.0 * home == c, slot, CAP + slot)
    shift = target - home
    shift = jnp.where(shift < 0.0, shift + SIDE, shift) - 1.0
    lane = lax.broadcasted_iota(jnp.int32, (TILES, LANES), 1).astype(jnp.float32)
    row = lax.broadcasted_iota(jnp.int32, (TILES, LANES), 0).astype(jnp.float32)
    perm = down(lane == target * CAP + pos, row)
    outgoing = jnp.where(moves & (home == x), SEND + shift * CAP + order, -1.0)
    group = jnp.floor(order * (1.0 / QUAD))
    arriving = 2 * CAP + group * 3 * QUAD + shift * QUAD + order - group * QUAD
    incoming = jnp.where(target == x, GATHER + pos, -1.0)
    table = down(lane == outgoing, place) + down(lane == incoming, jnp.where(moves, arriving, place))
    most = jnp.max(jnp.where(moves, order, -1.0), axis=0, keepdims=True)
    rounds = jnp.floor((most + QUAD) * (1.0 / QUAD))
    table = jnp.where(lane[:1] == ROUNDS, rounds, table)
    out[0:1, :] = perm.astype(jnp.int32)
    out[1:2, :] = table.astype(jnp.int32)


def make_plan(tile_owner):
    vmem = pl.BlockSpec(memory_space=pltpu.VMEM)
    return pl.pallas_call(
        plan_kernel,
        out_shape=jax.ShapeDtypeStruct((2, LANES), jnp.int32),
        in_specs=[vmem],
        out_specs=vmem,
        name="make_plan",
    )(tile_owner[None, :])


def amplitude_kernel(table, amp, after, *outs):
    x = lax.axis_index("x")
    load = lambda base: amp[:, pl.ds(base, WINDOW)].astype(jnp.float32)
    for s, out in enumerate(outs):
        first = ((x + s) % SIDE) * CAP
        for g in range(0, CAP, QUAD):
            starts = [table[0, first + g + j] * TW for j in range(QUAD)]
            for k, column in enumerate(four_tiles(load, starts, TILES * TW)):
                at = g * TW + k * LANES
                out[:, at : at + LANES] = column.astype(jnp.bfloat16)


def order_amplitudes(table, amplitudes, after):
    vmem = pl.BlockSpec(memory_space=pltpu.VMEM)
    return pl.pallas_call(
        amplitude_kernel,
        out_shape=tuple(jax.ShapeDtypeStruct((64, WIDTH), jnp.bfloat16) for _ in range(SIDE)),
        in_specs=[pl.BlockSpec(memory_space=pltpu.SMEM), vmem, pl.BlockSpec(memory_space=pl.ANY)],
        out_specs=tuple(vmem for _ in range(SIDE)),
        compiler_params=VMEM,
        name="order_amplitudes",
    )(table, amplitudes, after)


def tile_rows(pool, table, first, out, at):
    def rows(i, carry):
        here = pl.ds(pl.multiple_of(i * 48, 16), 48)
        load = lambda base: pool[here, pl.ds(base, WINDOW)].astype(jnp.float32)
        starts = [table[1, first + j] * TW for j in range(QUAD)]
        for k, column in enumerate(four_tiles(load, starts, pool.shape[1])):
            out[here, at + k * LANES : at + (k + 1) * LANES] = column.astype(jnp.bfloat16)
        return carry

    lax.fori_loop(0, HALF // 48, rows, 0)


def fill_pool(sources, pool, sems):
    half = pl.ds(pl.multiple_of(lax.axis_index("c") * HALF, 16), HALF)
    copies = []
    at = 0
    for i, ref in enumerate(sources):
        src = ref.at[half] if i < 2 else ref
        width = ref.shape[1]
        copies.append(pltpu.make_async_copy(src, pool.at[:, pl.ds(at, width)], sems.at[i]))
        at += width
    for copy in copies:
        copy.start()
    for copy in copies:
        copy.wait()


def pack_kernel(number, table, mine, other, after, out1, out2, out3, pool, sems):
    fill_pool((mine, other), pool, sems)
    for s, out in enumerate((out1, out2, out3)):
        tile_rows(pool, table, SEND + s * CAP + number * QUAD, out, 0)


def assemble_kernel(table, mine, other, in1, in2, in3, extra, out, pool, sems):
    fill_pool((mine, other, in1, in2, in3), pool, sems)
    at, width = 2 * WIDTH + 3 * QUAD * TW, QUAD * TW

    @pl.when(table[1, ROUNDS] > 1)
    def _():
        copies = [
            pltpu.make_async_copy(extra.at[i], pool.at[:, pl.ds(at + i * width, width)], sems.at[i])
            for i in range(extra.shape[0])
        ]
        for copy in copies:
            copy.start()
        for copy in copies:
            copy.wait()

    for g in range(CAP // QUAD):
        tile_rows(pool, table, GATHER + g * QUAD, out, g * QUAD * TW)


def pack(number, table, mine, other, after):
    anywhere = pl.BlockSpec(memory_space=pl.ANY)
    return pl.pallas_call(
        functools.partial(pack_kernel, number),
        out_shape=tuple(jax.ShapeDtypeStruct((HALF, QUAD * TW), jnp.bfloat16) for _ in range(3)),
        in_specs=[pl.BlockSpec(memory_space=pltpu.SMEM), anywhere, anywhere, anywhere],
        out_specs=tuple(pl.BlockSpec(memory_space=pltpu.VMEM) for _ in range(3)),
        scratch_shapes=[pltpu.VMEM((HALF, 2 * WIDTH), jnp.bfloat16), pltpu.SemaphoreType.DMA((2,))],
        compiler_params=VMEM,
        name="pack",
    )(table, mine, other, after)


def assemble(table, mine, other, received, extra):
    anywhere = pl.BlockSpec(memory_space=pl.ANY)
    n = len(received) + extra.shape[0]
    return pl.pallas_call(
        assemble_kernel,
        out_shape=jax.ShapeDtypeStruct((HALF, WIDTH), jnp.bfloat16),
        in_specs=[pl.BlockSpec(memory_space=pltpu.SMEM)] + [anywhere] * 6,
        out_specs=pl.BlockSpec(memory_space=pltpu.VMEM),
        scratch_shapes=[
            pltpu.VMEM((HALF, 2 * WIDTH + n * QUAD * TW), jnp.bfloat16),
            pltpu.SemaphoreType.DMA((2 + n,)),
        ],
        compiler_params=VMEM,
        cost_estimate=pl.CostEstimate(flops=0, bytes_accessed=10 << 20, transcendentals=0),
        name="assemble",
    )(table, mine, other, *received, extra)


def send(packed):
    return [ring(part, "x", s + 1) for s, part in enumerate(packed)]


def later_rounds(table, mine, other):
    def more(table, mine, other):
        parts = []
        for number in range(1, CAP // QUAD):
            parts += send(pack(number, table, mine, other, parts[-1] if parts else table))
        return jnp.stack(parts)

    def none(table, mine, other):
        return jnp.zeros((3 * (CAP // QUAD - 1), HALF, QUAD * TW), mine.dtype)

    return lax.cond(table[1, ROUNDS] > 1, more, none, table, mine, other)


def encode(value):
    top = jnp.max(jnp.abs(value), axis=1, keepdims=True)
    code = jnp.ceil(jnp.log2(jnp.maximum(top, 1e-33)) * STEPS)
    level = jnp.floor(value * (jnp.exp2(code * (-1.0 / STEPS)) * LEVELS) + 0.5)
    return level.astype(jnp.int32).astype(jnp.int16), code.astype(jnp.int32).astype(jnp.int16)


def decode(coded):
    wide = coded.astype(jnp.int32).astype(jnp.float32)
    lane = lax.broadcasted_iota(jnp.int32, wide.shape, 1)
    code = jnp.sum(jnp.where(lane == HALF, wide, 0.0), axis=1, keepdims=True)
    return wide[:, :HALF] * (jnp.exp2(code * (1.0 / STEPS)) * (1.0 / LEVELS))


def put(out, k, level, code):
    out[k, :, :HALF] = level
    out[k, :, HALF:] = jnp.broadcast_to(code, (64, PADDED - HALF))


def code_far_kernel(n, *refs):
    for k in range(n):
        put(refs[n], k, *encode(refs[k][...]))


def code_near_kernel(n, *refs):
    sums, (arrived, nxt, prv) = refs[: 2 * n], refs[2 * n :]
    c = lax.axis_index("c")

    def run(first, out, other_first, other_out):
        for k in range(n):
            put(out, k, *encode(sums[first + k][...] + decode(arrived[k])))
        for k in range(n):
            put(other_out, k, *encode(sums[other_first + k][...]))

    pl.when(c == 0)(lambda: run(0, nxt, n, prv))
    pl.when(c != 0)(lambda: run(n, prv, 0, nxt))


def code_last_kernel(n, *refs):
    sums, (low, high, _, out) = refs[:n], refs[n:]
    for k in range(n):
        level, code = encode(sums[k][...] + decode(low[k]) + decode(high[k]))
        code = jnp.broadcast_to(code, (64, PADDED - HALF))
        for row in range(SIDE):
            rows = slice(16 * row, 16 * (row + 1))
            out[row, k, :, :HALF] = level[rows]
            out[row, k, :, HALF:] = code[rows]


def code_far(sums):
    n = len(sums)
    return pl.pallas_call(
        functools.partial(code_far_kernel, n),
        out_shape=jax.ShapeDtypeStruct((n, 2 * CUT, PADDED), jnp.int16),
        grid=(4,),
        in_specs=[pl.BlockSpec((64, HALF), lambda i: (i, 0))] * n,
        out_specs=pl.BlockSpec((n, 64, PADDED), lambda i: (0, i, 0)),
        compiler_params=VMEM,
        name="code_far",
    )(*sums)


def code_near(sums_next, sums_prev, arrived):
    n = len(sums_next)
    out = jax.ShapeDtypeStruct((n, 2 * CUT, PADDED), jnp.int16)
    block = pl.BlockSpec((n, 64, PADDED), lambda i: (0, i, 0))
    return pl.pallas_call(
        functools.partial(code_near_kernel, n),
        out_shape=(out, out),
        grid=(4,),
        in_specs=[pl.BlockSpec((64, HALF), lambda i: (i, 0))] * (2 * n) + [block],
        out_specs=(block, block),
        compiler_params=VMEM,
        name="code_near",
    )(*sums_next, *sums_prev, arrived)


def code_last(sums, low, high, group, before):
    n = len(sums)
    block = pl.BlockSpec((n, 64, PADDED), lambda i: (0, i, 0))
    return pl.pallas_call(
        functools.partial(code_last_kernel, n),
        out_shape=jax.ShapeDtypeStruct((SIDE * SIDE, 2 * n, 16, PADDED), jnp.int16),
        grid=(4,),
        in_specs=[pl.BlockSpec((64, HALF), lambda i: (i, 0))] * n
        + [block, block, pl.BlockSpec(memory_space=pl.ANY)],
        out_specs=pl.BlockSpec((SIDE, n, 16, PADDED), lambda i: (i, group, 0, 0)),
        input_output_aliases={} if before is None else {n + 2: 0},
        compiler_params=VMEM,
        name="code_last",
    )(*sums, low, high, low if before is None else before)


def finish_kernel(groups, *refs):
    c = lax.axis_index("c")
    got, (virt, occ, out) = refs[: len(groups)], refs[len(groups) :]
    spots = {up: (ref, 2 * k) for ref, group in zip(got, groups) for k, up in enumerate(group)}
    by_zr = one_hot(64, lambda i: ((i // 4) % 4) * 16 + (i // 16) * 4 + i % 4).astype(jnp.float32)
    for ya in range(SIDE):
        for h in range(2):
            parts = []
            for ys in range(SIDE):
                ref, k = spots[(ya - ys) % SIDE]
                parts.append(ref[ys, k + jnp.bitwise_xor(c, h)])
            value = decode(jnp.concatenate(parts, axis=0))
            value = jnp.dot(by_zr, value, precision=lax.Precision.HIGHEST)
            j = 2 * ya + h
            out[:, j * HALF : (j + 1) * HALF] = value / (virt[j : j + 1, :HALF] - occ[...])


def finish(groups, got, virt, occ):
    block = lambda n: pl.BlockSpec((SIDE, n, 16, PADDED), lambda i: (i, 0, 0, 0))
    return pl.pallas_call(
        functools.partial(finish_kernel, groups),
        grid=(SIDE,),
        out_shape=jax.ShapeDtypeStruct((64, SIDE * WIDTH), jnp.float32),
        in_specs=[block(2 * len(group)) for group in groups]
        + [
            pl.BlockSpec((8, PADDED), lambda i: (i, 0)),
            pl.BlockSpec((64, 1), lambda i: (0, 0)),
        ],
        out_specs=pl.BlockSpec((64, WIDTH), lambda i: (0, i)),
        compiler_params=VMEM,
        name="finish",
    )(*got, virt, occ)


def ring_pieces(first, second):
    both = (first, second)
    steps = [ring(piece, axis, shift) for piece, axis, _ in both for shift in (1, -1)]
    steps = lax.optimization_barrier(tuple(steps))
    lows, highs = steps[0::2], steps[1::2]
    fars = []
    for (_, axis, cut), low, high in zip(both, lows, highs):
        fars += [ring(low[:cut], axis, 1), ring(high[cut:], axis, -1)]
    fars = lax.optimization_barrier(tuple(fars))
    return [
        (piece, high, *fars[2 * i : 2 * i + 2], low)
        for i, ((piece, _, _), low, high) in enumerate(zip(both, lows, highs))
    ]


def on_device(amplitudes, integrals, tile_ids, tile_owner, occ_pairs, occ_energy, vir_energy):
    z, y, x, c = (lax.axis_index(name) for name in ALL)
    occ_dev = amplitudes.shape[0]
    sub = occ_dev // (SIDE * SIDE)
    mine = integrals[0]
    other = swap(mine)
    table = make_plan(tile_owner)
    extra = later_rounds(table, mine, other)
    packed = pack(0, table, mine, other, extra)
    first = send(packed)
    last, *leaving = order_amplitudes(table, amplitudes, packed[0])
    prev, far, nxt = send(leaving)
    shard = assemble(table, mine, other, first, extra)
    arrived = jnp.concatenate([far, nxt, prev, last], axis=0)
    arrived, _ = lax.optimization_barrier((arrived, shard))
    shares, pieces = ring_pieces((shard, "y", CUT), (arrived, "z", 2 * occ_dev))
    own, high, far0, far1, low = [(piece, swap(piece)) for piece in shares]
    both = tuple(jnp.concatenate([far0[i], far1[i]], axis=0) for i in range(2))
    blocks = [own, high, both, low]
    by_k = one_hot(256, lambda i: (((i // 4) % 4 - z) % 4) * 64 + (i // 16) * 4 + i % 4)

    def pairs_of(number):
        own, high, far0, far1, low = pieces
        at = lambda p, n: p[n * occ_dev : (n + 1) * occ_dev]
        far = at(far0, number) if number < 2 else at(far1, number - 2)
        whole = jnp.concatenate([at(own, number), at(high, number), far, at(low, number)], axis=0)
        return jnp.dot(by_k, whole, preferred_element_type=jnp.float32).astype(whole.dtype)

    def product(a, b):
        return lax.dot_general(a, b, (((1,), (1,)), ((), ())), preferred_element_type=jnp.float32)

    def sums(number, blocks):
        return [product(pairs[number], b) for b in blocks]

    pairs = [pairs_of(number) for number in range(SIDE)]

    def near_sums(next_pairs, prev_pairs, *blocks):
        return [product(p, b) for p in (next_pairs, prev_pairs) for b in blocks]

    def no_sums(next_pairs, prev_pairs, *blocks):
        return [jnp.zeros((4 * occ_dev, HALF), jnp.float32) for _ in range(2 * len(blocks))]

    groups = ((0, 1), (2, 3))
    parts = [[half for up in group for half in blocks[up]] for group in groups]
    sent = [code_far(sums(0, part)) for part in parts]
    pairs[1], pairs[2], pairs[3], *_ = lax.optimization_barrier((*pairs[1:], *sent))
    far_sums = [part_ring(value, value, "x") for value in sent]
    leaving, behind = [], pairs[1:3]
    for part, arriving in zip(parts, far_sums):
        both = lax.cond(table[1, ROUNDS] >= 0, near_sums, no_sums, *behind, *part)
        leaving.append(code_near(both[: len(part)], both[len(part) :], arriving))
        *behind, _, _ = lax.optimization_barrier((pairs[1], pairs[2], *leaving[-1]))
    near_arrived = [(ring(nxt, "x", 1), ring(prv, "x", -1)) for nxt, prv in leaving]
    pairs[3], *_ = lax.optimization_barrier((pairs[3], *leaving[-1]))
    last_sums = [sums(3, part) for part in parts]
    total = None
    for group, (sums_, arriving) in enumerate(zip(last_sums, near_arrived)):
        total = code_last(sums_, *arriving, group, total)
    got = lax.all_to_all(total, ("z", "y"), split_axis=0, concat_axis=0, tiled=True)
    sent = leaving[-1]
    occ_pairs, occ_energy, vir_energy, _ = lax.optimization_barrier(
        (occ_pairs, occ_energy, vir_energy, sent[0])
    )

    grid = occ_pairs.reshape(SIDE * SIDE, 2 * SIDE, SIDE * SIDE, sub, 2)
    here = lax.dynamic_slice(grid, (0, 2 * x + c, SIDE * z + y, 0, 0), (SIDE * SIDE, 1, 1, sub, 2))
    occ_sum = jnp.sum(jnp.take(occ_energy, here.reshape(occ_dev, 2), axis=0), axis=1)
    per_row = NVIR // TW
    second = jnp.take(vir_energy.reshape(per_row, TW), tile_ids % per_row, axis=0)
    virt_sum = (jnp.take(vir_energy, tile_ids // per_row)[:, None] + second).reshape(8 * SIDE, HALF)
    virt_sum = jnp.pad(virt_sum, ((0, 0), (0, PADDED - HALF)))
    return finish(((0, 1, 2, 3),), (got,), virt_sum, occ_sum[:, None])[None]


def solution(mesh):
    chips = Mesh(mesh.devices.reshape(SIDE, SIDE, SIDE, 2), ALL)
    placed = (P(ALL, None), P(("x", "c"), ("z", "y"), None), P(), P(), P(), P(), P())
    return jax.shard_map(
        on_device, mesh=chips, in_specs=placed, out_specs=P(("z", "y"), ("x", "c"), None), check_vma=False
    )
```

```python
import functools

import jax
import jax.numpy as jnp
from jax import lax
from jax.experimental import pallas as pl
from jax.experimental.pallas import tpu as pltpu
from jax.sharding import Mesh, PartitionSpec as P

TW = 96
NVIR = 2016
SIDE = 4
TILES = 80
CAP = 20
QUAD = 4
LANES = 128
WINDOW = 2 * LANES
HALF = 240
PADDED = 256
WIDTH = CAP * TW
CUT = 128
LEVELS = 32000.0
STEPS = 256.0
ALL = ("z", "y", "x", "c")
SEND = 0
GATHER = 3 * CAP
ROUNDS = GATHER + CAP
VMEM = pltpu.CompilerParams(vmem_limit_bytes=48 * 1024 * 1024)


def ring(value, axis, shift):
    return lax.ppermute(value, axis, [(i, (i + shift) % SIDE) for i in range(SIDE)])


def part_ring(up, down, axis):
    value = up if up is down else jnp.where(lax.axis_index("c") == 0, up, down)
    pairs = [(2 * i + c, 2 * ((i + 1 - 2 * c) % SIDE) + c) for i in range(SIDE) for c in range(2)]
    return lax.ppermute(value, (axis, "c"), pairs)


def swap(value):
    return lax.ppermute(value, "c", [(0, 1), (1, 0)])


def four_tiles(load, starts, limit):
    parts = []
    for start, want in zip(starts, (0, 96, 64, 160)):
        base = jnp.minimum((start // LANES) * LANES, limit - WINDOW)
        window = load(pl.multiple_of(base, LANES))
        parts.append(pltpu.roll(window, (want - (start - base)) & (WINDOW - 1), 1))
    a, b, c, d = parts
    lane = lax.broadcasted_iota(jnp.int32, (a.shape[0], LANES), 1)
    return (
        jnp.where(lane < 96, a[:, :LANES], b[:, :LANES]),
        jnp.where(lane < 64, b[:, LANES:], c[:, :LANES]),
        jnp.where(lane < 32, c[:, LANES:], d[:, LANES:]),
    )


def one_hot(size, source):
    row = lax.broadcasted_iota(jnp.int32, (size, size), 0)
    col = lax.broadcasted_iota(jnp.int32, (size, size), 1)
    return jnp.where(col == source(row), 1.0, 0.0).astype(jnp.bfloat16)


def plan_kernel(owner, out):
    x, c = (lax.axis_index(name).astype(jnp.float32) for name in "xc")
    i = lax.broadcasted_iota(jnp.int32, (TILES, TILES), 0)
    j = lax.broadcasted_iota(jnp.int32, (TILES, TILES), 1)
    across = lambda mask, value=1.0: jnp.sum(jnp.where(mask, value, 0.0), axis=1, keepdims=True)
    down = lambda mask, value=1.0: jnp.sum(jnp.where(mask, value, 0.0), axis=0, keepdims=True)
    earlier = j < i
    owner_row = owner[...].astype(jnp.float32)
    owner_col = across(i == j, owner_row)
    home_row, home = jnp.floor(owner_row * 0.5), jnp.floor(owner_col * 0.5)
    slot = across((owner_row == owner_col) & earlier)
    rank = across((home_row == home) & earlier)
    moves = rank >= CAP
    over = under = jnp.zeros((1, 1), jnp.float32)
    number = rank - CAP
    ends, starts = [], []
    for k in range(SIDE):
        load = across(home_row == k)
        number = number + jnp.where(home == k, over, 0.0)
        starts.append(load - under)
        over = over + jnp.maximum(load - CAP, 0.0)
        under = under + jnp.maximum(CAP - load, 0.0)
        ends.append(under)
    target = jnp.where(moves, sum(jnp.where(number >= end, 1.0, 0.0) for end in ends), home)
    start = sum(jnp.where(target == k, starts[k], 0.0) for k in range(SIDE))
    pos = jnp.where(moves, start + number, rank)
    moving = jnp.where(moves, home * SIDE + target, -1.0)
    order = across((down(i == j, moving) == moving) & earlier)
    place = jnp.where(owner_col - 2.0 * home == c, slot, CAP + slot)
    shift = target - home
    shift = jnp.where(shift < 0.0, shift + SIDE, shift) - 1.0
    lane = lax.broadcasted_iota(jnp.int32, (TILES, LANES), 1).astype(jnp.float32)
    row = lax.broadcasted_iota(jnp.int32, (TILES, LANES), 0).astype(jnp.float32)
    perm = down(lane == target * CAP + pos, row)
    outgoing = jnp.where(moves & (home == x), SEND + shift * CAP + order, -1.0)
    group = jnp.floor(order * (1.0 / QUAD))
    arriving = 2 * CAP + group * 3 * QUAD + shift * QUAD + order - group * QUAD
    incoming = jnp.where(target == x, GATHER + pos, -1.0)
    table = down(lane == outgoing, place) + down(lane == incoming, jnp.where(moves, arriving, place))
    most = jnp.max(jnp.where(moves, order, -1.0), axis=0, keepdims=True)
    rounds = jnp.floor((most + QUAD) * (1.0 / QUAD))
    table = jnp.where(lane[:1] == ROUNDS, rounds, table)
    out[0:1, :] = perm.astype(jnp.int32)
    out[1:2, :] = table.astype(jnp.int32)


def make_plan(tile_owner):
    vmem = pl.BlockSpec(memory_space=pltpu.VMEM)
    return pl.pallas_call(
        plan_kernel,
        out_shape=jax.ShapeDtypeStruct((2, LANES), jnp.int32),
        in_specs=[vmem],
        out_specs=vmem,
        name="make_plan",
    )(tile_owner[None, :])


def amplitude_kernel(table, amp, after, *outs):
    x = lax.axis_index("x")
    load = lambda base: amp[:, pl.ds(base, WINDOW)].astype(jnp.float32)
    for s, out in enumerate(outs):
        first = ((x + s) % SIDE) * CAP

        def four(g, carry, first=first, out=out):
            starts = [table[0, first + QUAD * g + j] * TW for j in range(QUAD)]
            for k, column in enumerate(four_tiles(load, starts, TILES * TW)):
                at = pl.multiple_of(g * QUAD * TW + k * LANES, LANES)
                out[:, pl.ds(at, LANES)] = column.astype(jnp.bfloat16)
            return carry

        lax.fori_loop(0, CAP // QUAD, four, 0)


def order_amplitudes(table, amplitudes, after):
    vmem = pl.BlockSpec(memory_space=pltpu.VMEM)
    return pl.pallas_call(
        amplitude_kernel,
        out_shape=tuple(jax.ShapeDtypeStruct((64, WIDTH), jnp.bfloat16) for _ in range(SIDE)),
        in_specs=[pl.BlockSpec(memory_space=pltpu.SMEM), vmem, pl.BlockSpec(memory_space=pl.ANY)],
        out_specs=tuple(vmem for _ in range(SIDE)),
        compiler_params=VMEM,
        name="order_amplitudes",
    )(table, amplitudes, after)


def tile_rows(pool, table, first, out, at):
    def rows(i, carry):
        here = pl.ds(pl.multiple_of(i * 48, 16), 48)
        load = lambda base: pool[here, pl.ds(base, WINDOW)].astype(jnp.float32)
        starts = [table[1, first + j] * TW for j in range(QUAD)]
        for k, column in enumerate(four_tiles(load, starts, pool.shape[1])):
            out[here, pl.ds(pl.multiple_of(at + k * LANES, LANES), LANES)] = column.astype(jnp.bfloat16)
        return carry

    lax.fori_loop(0, HALF // 48, rows, 0)


def fill_pool(sources, pool, sems):
    half = pl.ds(pl.multiple_of(lax.axis_index("c") * HALF, 16), HALF)
    copies = []
    at = 0
    for i, ref in enumerate(sources):
        src = ref.at[half] if i < 2 else ref
        width = ref.shape[1]
        copies.append(pltpu.make_async_copy(src, pool.at[:, pl.ds(at, width)], sems.at[i]))
        at += width
    for copy in copies:
        copy.start()
    for copy in copies:
        copy.wait()


def pack_kernel(number, table, mine, other, after, out1, out2, out3, pool, sems):
    fill_pool((mine, other), pool, sems)
    for s, out in enumerate((out1, out2, out3)):
        tile_rows(pool, table, SEND + s * CAP + number * QUAD, out, 0)


def assemble_kernel(table, mine, other, in1, in2, in3, extra, out, pool, sems):
    fill_pool((mine, other, in1, in2, in3), pool, sems)
    at, width = 2 * WIDTH + 3 * QUAD * TW, QUAD * TW

    @pl.when(table[1, ROUNDS] > 1)
    def _():
        copies = [
            pltpu.make_async_copy(extra.at[i], pool.at[:, pl.ds(at + i * width, width)], sems.at[i])
            for i in range(extra.shape[0])
        ]
        for copy in copies:
            copy.start()
        for copy in copies:
            copy.wait()

    def four(g, carry):
        tile_rows(pool, table, GATHER + g * QUAD, out, g * QUAD * TW)
        return carry

    lax.fori_loop(0, CAP // QUAD, four, 0)


def pack(number, table, mine, other, after):
    anywhere = pl.BlockSpec(memory_space=pl.ANY)
    return pl.pallas_call(
        functools.partial(pack_kernel, number),
        out_shape=tuple(jax.ShapeDtypeStruct((HALF, QUAD * TW), jnp.bfloat16) for _ in range(3)),
        in_specs=[pl.BlockSpec(memory_space=pltpu.SMEM), anywhere, anywhere, anywhere],
        out_specs=tuple(pl.BlockSpec(memory_space=pltpu.VMEM) for _ in range(3)),
        scratch_shapes=[pltpu.VMEM((HALF, 2 * WIDTH), jnp.bfloat16), pltpu.SemaphoreType.DMA((2,))],
        compiler_params=VMEM,
        name="pack",
    )(table, mine, other, after)


def assemble(table, mine, other, received, extra):
    anywhere = pl.BlockSpec(memory_space=pl.ANY)
    n = len(received) + extra.shape[0]
    return pl.pallas_call(
        assemble_kernel,
        out_shape=jax.ShapeDtypeStruct((HALF, WIDTH), jnp.bfloat16),
        in_specs=[pl.BlockSpec(memory_space=pltpu.SMEM)] + [anywhere] * 6,
        out_specs=pl.BlockSpec(memory_space=pltpu.VMEM),
        scratch_shapes=[
            pltpu.VMEM((HALF, 2 * WIDTH + n * QUAD * TW), jnp.bfloat16),
            pltpu.SemaphoreType.DMA((2 + n,)),
        ],
        compiler_params=VMEM,
        cost_estimate=pl.CostEstimate(flops=0, bytes_accessed=10 << 20, transcendentals=0),
        name="assemble",
    )(table, mine, other, *received, extra)


def send(packed):
    return [ring(part, "x", s + 1) for s, part in enumerate(packed)]


def later_rounds(table, mine, other):
    def more(table, mine, other):
        parts = []
        for number in range(1, CAP // QUAD):
            parts += send(pack(number, table, mine, other, parts[-1] if parts else table))
        return jnp.stack(parts)

    def none(table, mine, other):
        return jnp.zeros((3 * (CAP // QUAD - 1), HALF, QUAD * TW), mine.dtype)

    return lax.cond(table[1, ROUNDS] > 1, more, none, table, mine, other)


def encode(value):
    top = jnp.max(jnp.abs(value), axis=1, keepdims=True)
    code = jnp.ceil(jnp.log2(jnp.maximum(top, 1e-33)) * STEPS)
    level = jnp.floor(value * (jnp.exp2(code * (-1.0 / STEPS)) * LEVELS) + 0.5)
    return level.astype(jnp.int32).astype(jnp.int16), code.astype(jnp.int32).astype(jnp.int16)


def decode(coded):
    wide = coded.astype(jnp.int32).astype(jnp.float32)
    lane = lax.broadcasted_iota(jnp.int32, wide.shape, 1)
    code = jnp.sum(jnp.where(lane == HALF, wide, 0.0), axis=1, keepdims=True)
    return wide[:, :HALF] * (jnp.exp2(code * (1.0 / STEPS)) * (1.0 / LEVELS))


def put(out, k, level, code):
    out[k, :, :HALF] = level
    out[k, :, HALF:] = jnp.broadcast_to(code, (64, PADDED - HALF))


def code_far_kernel(n, *refs):
    for k in range(n):
        put(refs[n], k, *encode(refs[k][...]))


def code_near_kernel(n, *refs):
    sums, (arrived, nxt, prv) = refs[: 2 * n], refs[2 * n :]
    c = lax.axis_index("c")

    def run(first, out, other_first, other_out):
        for k in range(n):
            put(out, k, *encode(sums[first + k][...] + decode(arrived[k])))
        for k in range(n):
            put(other_out, k, *encode(sums[other_first + k][...]))

    pl.when(c == 0)(lambda: run(0, nxt, n, prv))
    pl.when(c != 0)(lambda: run(n, prv, 0, nxt))


def code_last_kernel(n, *refs):
    sums, (low, high, _, out) = refs[:n], refs[n:]
    for k in range(n):
        level, code = encode(sums[k][...] + decode(low[k]) + decode(high[k]))
        code = jnp.broadcast_to(code, (64, PADDED - HALF))
        for row in range(SIDE):
            rows = slice(16 * row, 16 * (row + 1))
            out[row, k, :, :HALF] = level[rows]
            out[row, k, :, HALF:] = code[rows]


def code_far(sums):
    n = len(sums)
    return pl.pallas_call(
        functools.partial(code_far_kernel, n),
        out_shape=jax.ShapeDtypeStruct((n, 2 * CUT, PADDED), jnp.int16),
        grid=(4,),
        in_specs=[pl.BlockSpec((64, HALF), lambda i: (i, 0))] * n,
        out_specs=pl.BlockSpec((n, 64, PADDED), lambda i: (0, i, 0)),
        compiler_params=VMEM,
        name="code_far",
    )(*sums)


def code_near(sums_next, sums_prev, arrived):
    n = len(sums_next)
    out = jax.ShapeDtypeStruct((n, 2 * CUT, PADDED), jnp.int16)
    block = pl.BlockSpec((n, 64, PADDED), lambda i: (0, i, 0))
    return pl.pallas_call(
        functools.partial(code_near_kernel, n),
        out_shape=(out, out),
        grid=(4,),
        in_specs=[pl.BlockSpec((64, HALF), lambda i: (i, 0))] * (2 * n) + [block],
        out_specs=(block, block),
        compiler_params=VMEM,
        name="code_near",
    )(*sums_next, *sums_prev, arrived)


def code_last(sums, low, high, group, before):
    n = len(sums)
    block = pl.BlockSpec((n, 64, PADDED), lambda i: (0, i, 0))
    return pl.pallas_call(
        functools.partial(code_last_kernel, n),
        out_shape=jax.ShapeDtypeStruct((SIDE * SIDE, 2 * n, 16, PADDED), jnp.int16),
        grid=(4,),
        in_specs=[pl.BlockSpec((64, HALF), lambda i: (i, 0))] * n
        + [block, block, pl.BlockSpec(memory_space=pl.ANY)],
        out_specs=pl.BlockSpec((SIDE, n, 16, PADDED), lambda i: (i, group, 0, 0)),
        input_output_aliases={} if before is None else {n + 2: 0},
        compiler_params=VMEM,
        name="code_last",
    )(*sums, low, high, low if before is None else before)


def finish_kernel(groups, *refs):
    c = lax.axis_index("c")
    got, (virt, occ, out) = refs[: len(groups)], refs[len(groups) :]
    spots = {up: (ref, 2 * k) for ref, group in zip(got, groups) for k, up in enumerate(group)}
    by_zr = one_hot(64, lambda i: ((i // 4) % 4) * 16 + (i // 16) * 4 + i % 4).astype(jnp.float32)
    for ya in range(SIDE):
        for h in range(2):
            parts = []
            for ys in range(SIDE):
                ref, k = spots[(ya - ys) % SIDE]
                parts.append(ref[ys, k + jnp.bitwise_xor(c, h)])
            value = decode(jnp.concatenate(parts, axis=0))
            value = jnp.dot(by_zr, value, precision=lax.Precision.HIGHEST)
            j = 2 * ya + h
            out[:, j * HALF : (j + 1) * HALF] = value / (virt[j : j + 1, :HALF] - occ[...])


def finish(groups, got, virt, occ):
    block = lambda n: pl.BlockSpec((SIDE, n, 16, PADDED), lambda i: (i, 0, 0, 0))
    return pl.pallas_call(
        functools.partial(finish_kernel, groups),
        grid=(SIDE,),
        out_shape=jax.ShapeDtypeStruct((64, SIDE * WIDTH), jnp.float32),
        in_specs=[block(2 * len(group)) for group in groups]
        + [
            pl.BlockSpec((8, PADDED), lambda i: (i, 0)),
            pl.BlockSpec((64, 1), lambda i: (0, 0)),
        ],
        out_specs=pl.BlockSpec((64, WIDTH), lambda i: (0, i)),
        compiler_params=VMEM,
        name="finish",
    )(*got, virt, occ)


def ring_pieces(first, second):
    both = (first, second)
    steps = [ring(piece, axis, shift) for piece, axis, _ in both for shift in (1, -1)]
    steps = lax.optimization_barrier(tuple(steps))
    lows, highs = steps[0::2], steps[1::2]
    fars = []
    for (_, axis, cut), low, high in zip(both, lows, highs):
        fars += [ring(low[:cut], axis, 1), ring(high[cut:], axis, -1)]
    fars = lax.optimization_barrier(tuple(fars))
    return [
        (piece, high, *fars[2 * i : 2 * i + 2], low)
        for i, ((piece, _, _), low, high) in enumerate(zip(both, lows, highs))
    ]


def on_device(amplitudes, integrals, tile_ids, tile_owner, occ_pairs, occ_energy, vir_energy):
    z, y, x, c = (lax.axis_index(name) for name in ALL)
    occ_dev = amplitudes.shape[0]
    sub = occ_dev // (SIDE * SIDE)
    mine = integrals[0]
    other = swap(mine)
    table = make_plan(tile_owner)
    extra = later_rounds(table, mine, other)
    packed = pack(0, table, mine, other, extra)
    first = send(packed)
    last, *leaving = order_amplitudes(table, amplitudes, packed[0])
    prev, far, nxt = send(leaving)
    shard = assemble(table, mine, other, first, extra)
    arrived = jnp.concatenate([far, nxt, prev, last], axis=0)
    arrived, _ = lax.optimization_barrier((arrived, shard))
    shares, pieces = ring_pieces((shard, "y", CUT), (arrived, "z", 2 * occ_dev))
    own, high, far0, far1, low = [(piece, swap(piece)) for piece in shares]
    both = tuple(jnp.concatenate([far0[i], far1[i]], axis=0) for i in range(2))
    blocks = [own, high, both, low]
    by_k = one_hot(256, lambda i: (((i // 4) % 4 - z) % 4) * 64 + (i // 16) * 4 + i % 4)

    def pairs_of(number):
        own, high, far0, far1, low = pieces
        at = lambda p, n: p[n * occ_dev : (n + 1) * occ_dev]
        far = at(far0, number) if number < 2 else at(far1, number - 2)
        whole = jnp.concatenate([at(own, number), at(high, number), far, at(low, number)], axis=0)
        return jnp.dot(by_k, whole, preferred_element_type=jnp.float32).astype(whole.dtype)

    def product(a, b):
        return lax.dot_general(a, b, (((1,), (1,)), ((), ())), preferred_element_type=jnp.float32)

    def sums(number, blocks):
        return [product(pairs[number], b) for b in blocks]

    pairs = [pairs_of(number) for number in range(SIDE)]

    def near_sums(next_pairs, prev_pairs, *blocks):
        return [product(p, b) for p in (next_pairs, prev_pairs) for b in blocks]

    def no_sums(next_pairs, prev_pairs, *blocks):
        return [jnp.zeros((4 * occ_dev, HALF), jnp.float32) for _ in range(2 * len(blocks))]

    groups = ((0, 1), (2, 3))
    parts = [[half for up in group for half in blocks[up]] for group in groups]
    sent = [code_far(sums(0, part)) for part in parts]
    pairs[1], pairs[2], pairs[3], *_ = lax.optimization_barrier((*pairs[1:], *sent))
    far_sums = [part_ring(value, value, "x") for value in sent]
    leaving, behind = [], pairs[1:3]
    for part, arriving in zip(parts, far_sums):
        both = lax.cond(table[1, ROUNDS] >= 0, near_sums, no_sums, *behind, *part)
        leaving.append(code_near(both[: len(part)], both[len(part) :], arriving))
        *behind, _, _ = lax.optimization_barrier((pairs[1], pairs[2], *leaving[-1]))
    near_arrived = [(ring(nxt, "x", 1), ring(prv, "x", -1)) for nxt, prv in leaving]
    pairs[3], *_ = lax.optimization_barrier((pairs[3], *leaving[-1]))
    last_sums = [sums(3, part) for part in parts]
    total = None
    for group, (sums_, arriving) in enumerate(zip(last_sums, near_arrived)):
        total = code_last(sums_, *arriving, group, total)
    got = lax.all_to_all(total, ("z", "y"), split_axis=0, concat_axis=0, tiled=True)
    sent = leaving[-1]
    occ_pairs, occ_energy, vir_energy, _ = lax.optimization_barrier(
        (occ_pairs, occ_energy, vir_energy, sent[0])
    )

    grid = occ_pairs.reshape(SIDE * SIDE, 2 * SIDE, SIDE * SIDE, sub, 2)
    here = lax.dynamic_slice(grid, (0, 2 * x + c, SIDE * z + y, 0, 0), (SIDE * SIDE, 1, 1, sub, 2))
    occ_sum = jnp.sum(jnp.take(occ_energy, here.reshape(occ_dev, 2), axis=0), axis=1)
    per_row = NVIR // TW
    second = jnp.take(vir_energy.reshape(per_row, TW), tile_ids % per_row, axis=0)
    virt_sum = (jnp.take(vir_energy, tile_ids // per_row)[:, None] + second).reshape(8 * SIDE, HALF)
    virt_sum = jnp.pad(virt_sum, ((0, 0), (0, PADDED - HALF)))
    return finish(((0, 1, 2, 3),), (got,), virt_sum, occ_sum[:, None])[None]


def solution(mesh):
    chips = Mesh(mesh.devices.reshape(SIDE, SIDE, SIDE, 2), ALL)
    placed = (P(ALL, None), P(("x", "c"), ("z", "y"), None), P(), P(), P(), P(), P())
    return jax.shard_map(
        on_device, mesh=chips, in_specs=placed, out_specs=P(("z", "y"), ("x", "c"), None), check_vma=False
    )
```

```python
import functools

import jax
import jax.numpy as jnp
from jax import lax
from jax.experimental import pallas as pl
from jax.experimental.pallas import tpu as pltpu
from jax.sharding import Mesh, PartitionSpec as P

TW = 96
NVIR = 2016
SIDE = 4
TILES = 80
CAP = 20
QUAD = 4
LANES = 128
WINDOW = 2 * LANES
HALF = 240
PADDED = 256
WIDTH = CAP * TW
CUT = 128
LEVELS = 32000.0
STEPS = 256.0
ALL = ("z", "y", "x", "c")
SEND = 0
GATHER = 3 * CAP
ROUNDS = GATHER + CAP
VMEM = pltpu.CompilerParams(vmem_limit_bytes=48 * 1024 * 1024)


def ring(value, axis, shift):
    return lax.ppermute(value, axis, [(i, (i + shift) % SIDE) for i in range(SIDE)])


def part_ring(up, down, axis):
    value = up if up is down else jnp.where(lax.axis_index("c") == 0, up, down)
    pairs = [(2 * i + c, 2 * ((i + 1 - 2 * c) % SIDE) + c) for i in range(SIDE) for c in range(2)]
    return lax.ppermute(value, (axis, "c"), pairs)


def swap(value):
    return lax.ppermute(value, "c", [(0, 1), (1, 0)])


def four_tiles(load, starts, limit):
    parts = []
    for start, want in zip(starts, (0, 96, 64, 160)):
        base = jnp.minimum((start // LANES) * LANES, limit - WINDOW)
        window = load(pl.multiple_of(base, LANES))
        parts.append(pltpu.roll(window, (want - (start - base)) & (WINDOW - 1), 1))
    a, b, c, d = parts
    lane = lax.broadcasted_iota(jnp.int32, (a.shape[0], LANES), 1)
    return (
        jnp.where(lane < 96, a[:, :LANES], b[:, :LANES]),
        jnp.where(lane < 64, b[:, LANES:], c[:, :LANES]),
        jnp.where(lane < 32, c[:, LANES:], d[:, LANES:]),
    )


def one_hot(size, source):
    row = lax.broadcasted_iota(jnp.int32, (size, size), 0)
    col = lax.broadcasted_iota(jnp.int32, (size, size), 1)
    return jnp.where(col == source(row), 1.0, 0.0).astype(jnp.bfloat16)


def plan_kernel(owner, out):
    x, c = (lax.axis_index(name).astype(jnp.float32) for name in "xc")
    i = lax.broadcasted_iota(jnp.int32, (TILES, TILES), 0)
    j = lax.broadcasted_iota(jnp.int32, (TILES, TILES), 1)
    across = lambda mask, value=1.0: jnp.sum(jnp.where(mask, value, 0.0), axis=1, keepdims=True)
    down = lambda mask, value=1.0: jnp.sum(jnp.where(mask, value, 0.0), axis=0, keepdims=True)
    earlier = j < i
    owner_row = owner[...].astype(jnp.float32)
    owner_col = across(i == j, owner_row)
    home_row, home = jnp.floor(owner_row * 0.5), jnp.floor(owner_col * 0.5)
    slot = across((owner_row == owner_col) & earlier)
    rank = across((home_row == home) & earlier)
    moves = rank >= CAP
    over = under = jnp.zeros((1, 1), jnp.float32)
    number = rank - CAP
    ends, starts = [], []
    for k in range(SIDE):
        load = across(home_row == k)
        number = number + jnp.where(home == k, over, 0.0)
        starts.append(load - under)
        over = over + jnp.maximum(load - CAP, 0.0)
        under = under + jnp.maximum(CAP - load, 0.0)
        ends.append(under)
    target = jnp.where(moves, sum(jnp.where(number >= end, 1.0, 0.0) for end in ends), home)
    start = sum(jnp.where(target == k, starts[k], 0.0) for k in range(SIDE))
    pos = jnp.where(moves, start + number, rank)
    moving = jnp.where(moves, home * SIDE + target, -1.0)
    order = across((down(i == j, moving) == moving) & earlier)
    place = jnp.where(owner_col - 2.0 * home == c, slot, CAP + slot)
    shift = target - home
    shift = jnp.where(shift < 0.0, shift + SIDE, shift) - 1.0
    lane = lax.broadcasted_iota(jnp.int32, (TILES, LANES), 1).astype(jnp.float32)
    row = lax.broadcasted_iota(jnp.int32, (TILES, LANES), 0).astype(jnp.float32)
    perm = down(lane == target * CAP + pos, row)
    outgoing = jnp.where(moves & (home == x), SEND + shift * CAP + order, -1.0)
    group = jnp.floor(order * (1.0 / QUAD))
    arriving = 2 * CAP + group * 3 * QUAD + shift * QUAD + order - group * QUAD
    incoming = jnp.where(target == x, GATHER + pos, -1.0)
    table = down(lane == outgoing, place) + down(lane == incoming, jnp.where(moves, arriving, place))
    most = jnp.max(jnp.where(moves, order, -1.0), axis=0, keepdims=True)
    rounds = jnp.floor((most + QUAD) * (1.0 / QUAD))
    table = jnp.where(lane[:1] == ROUNDS, rounds, table)
    out[0:1, :] = perm.astype(jnp.int32)
    out[1:2, :] = table.astype(jnp.int32)


def make_plan(tile_owner):
    vmem = pl.BlockSpec(memory_space=pltpu.VMEM)
    return pl.pallas_call(
        plan_kernel,
        out_shape=jax.ShapeDtypeStruct((2, LANES), jnp.int32),
        in_specs=[vmem],
        out_specs=vmem,
        name="make_plan",
    )(tile_owner[None, :])


def amplitude_kernel(table, amp, after, *outs):
    x = lax.axis_index("x")
    load = lambda base: amp[:, pl.ds(base, WINDOW)].astype(jnp.float32)
    for s, out in enumerate(outs):
        first = ((x + s) % SIDE) * CAP

        def four(g, carry, first=first, out=out):
            starts = [table[0, first + QUAD * g + j] * TW for j in range(QUAD)]
            for k, column in enumerate(four_tiles(load, starts, TILES * TW)):
                at = pl.multiple_of(g * QUAD * TW + k * LANES, LANES)
                out[:, pl.ds(at, LANES)] = column.astype(jnp.bfloat16)
            return carry

        lax.fori_loop(0, CAP // QUAD, four, 0)


def order_amplitudes(table, amplitudes, after):
    vmem = pl.BlockSpec(memory_space=pltpu.VMEM)
    return pl.pallas_call(
        amplitude_kernel,
        out_shape=tuple(jax.ShapeDtypeStruct((64, WIDTH), jnp.bfloat16) for _ in range(SIDE)),
        in_specs=[pl.BlockSpec(memory_space=pltpu.SMEM), vmem, pl.BlockSpec(memory_space=pl.ANY)],
        out_specs=tuple(vmem for _ in range(SIDE)),
        compiler_params=VMEM,
        name="order_amplitudes",
    )(table, amplitudes, after)


def tile_rows(pool, table, first, out, at):
    def rows(i, carry):
        here = pl.ds(pl.multiple_of(i * 48, 16), 48)
        load = lambda base: pool[here, pl.ds(base, WINDOW)].astype(jnp.float32)
        starts = [table[1, first + j] * TW for j in range(QUAD)]
        for k, column in enumerate(four_tiles(load, starts, pool.shape[1])):
            out[here, pl.ds(pl.multiple_of(at + k * LANES, LANES), LANES)] = column.astype(jnp.bfloat16)
        return carry

    lax.fori_loop(0, HALF // 48, rows, 0)


def fill_pool(sources, pool, sems):
    half = pl.ds(pl.multiple_of(lax.axis_index("c") * HALF, 16), HALF)
    copies = []
    at = 0
    for i, ref in enumerate(sources):
        src = ref.at[half] if i < 2 else ref
        width = ref.shape[1]
        copies.append(pltpu.make_async_copy(src, pool.at[:, pl.ds(at, width)], sems.at[i]))
        at += width
    for copy in copies:
        copy.start()
    for copy in copies:
        copy.wait()


def pack_kernel(number, table, mine, other, after, out1, out2, out3, pool, sems):
    fill_pool((mine, other), pool, sems)
    for s, out in enumerate((out1, out2, out3)):
        tile_rows(pool, table, SEND + s * CAP + number * QUAD, out, 0)


def assemble_kernel(table, mine, other, in1, in2, in3, extra, out, pool, sems):
    fill_pool((mine, other, in1, in2, in3), pool, sems)
    at, width = 2 * WIDTH + 3 * QUAD * TW, QUAD * TW

    @pl.when(table[1, ROUNDS] > 1)
    def _():
        copies = [
            pltpu.make_async_copy(extra.at[i], pool.at[:, pl.ds(at + i * width, width)], sems.at[i])
            for i in range(extra.shape[0])
        ]
        for copy in copies:
            copy.start()
        for copy in copies:
            copy.wait()

    def four(g, carry):
        tile_rows(pool, table, GATHER + g * QUAD, out, g * QUAD * TW)
        return carry

    lax.fori_loop(0, CAP // QUAD, four, 0)


def pack(number, table, mine, other, after):
    anywhere = pl.BlockSpec(memory_space=pl.ANY)
    return pl.pallas_call(
        functools.partial(pack_kernel, number),
        out_shape=tuple(jax.ShapeDtypeStruct((HALF, QUAD * TW), jnp.bfloat16) for _ in range(3)),
        in_specs=[pl.BlockSpec(memory_space=pltpu.SMEM), anywhere, anywhere, anywhere],
        out_specs=tuple(pl.BlockSpec(memory_space=pltpu.VMEM) for _ in range(3)),
        scratch_shapes=[pltpu.VMEM((HALF, 2 * WIDTH), jnp.bfloat16), pltpu.SemaphoreType.DMA((2,))],
        compiler_params=VMEM,
        name="pack",
    )(table, mine, other, after)


def assemble(table, mine, other, received, extra):
    anywhere = pl.BlockSpec(memory_space=pl.ANY)
    n = len(received) + extra.shape[0]
    return pl.pallas_call(
        assemble_kernel,
        out_shape=jax.ShapeDtypeStruct((HALF, WIDTH), jnp.bfloat16),
        in_specs=[pl.BlockSpec(memory_space=pltpu.SMEM)] + [anywhere] * 6,
        out_specs=pl.BlockSpec(memory_space=pltpu.VMEM),
        scratch_shapes=[
            pltpu.VMEM((HALF, 2 * WIDTH + n * QUAD * TW), jnp.bfloat16),
            pltpu.SemaphoreType.DMA((2 + n,)),
        ],
        compiler_params=VMEM,
        cost_estimate=pl.CostEstimate(flops=0, bytes_accessed=10 << 20, transcendentals=0),
        name="assemble",
    )(table, mine, other, *received, extra)


def send(packed):
    return [ring(part, "x", s + 1) for s, part in enumerate(packed)]


def later_rounds(table, mine, other):
    def more(table, mine, other):
        parts = []
        for number in range(1, CAP // QUAD):
            parts += send(pack(number, table, mine, other, parts[-1] if parts else table))
        return jnp.stack(parts)

    def none(table, mine, other):
        return pl.pallas_call(
            lambda out: None,
            out_shape=jax.ShapeDtypeStruct((3 * (CAP // QUAD - 1), HALF, QUAD * TW), mine.dtype),
            out_specs=pl.BlockSpec(memory_space=pl.ANY),
            name="unused",
        )()

    return lax.cond(table[1, ROUNDS] > 1, more, none, table, mine, other)


def encode(value):
    top = jnp.max(jnp.abs(value), axis=1, keepdims=True)
    code = jnp.ceil(jnp.log2(jnp.maximum(top, 1e-33)) * STEPS)
    level = jnp.floor(value * (jnp.exp2(code * (-1.0 / STEPS)) * LEVELS) + 0.5)
    return level.astype(jnp.int32).astype(jnp.int16), code.astype(jnp.int32).astype(jnp.int16)


def decode(coded):
    wide = coded.astype(jnp.int32).astype(jnp.float32)
    lane = lax.broadcasted_iota(jnp.int32, wide.shape, 1)
    code = jnp.sum(jnp.where(lane == HALF, wide, 0.0), axis=1, keepdims=True)
    return wide[:, :HALF] * (jnp.exp2(code * (1.0 / STEPS)) * (1.0 / LEVELS))


def put(out, k, level, code):
    out[k, :, :HALF] = level
    out[k, :, HALF:] = jnp.broadcast_to(code, (64, PADDED - HALF))


def code_far_kernel(n, *refs):
    for k in range(n):
        put(refs[n], k, *encode(refs[k][...]))


def code_near_kernel(n, *refs):
    sums, (arrived, nxt, prv) = refs[: 2 * n], refs[2 * n :]
    c = lax.axis_index("c")

    def run(first, out, other_first, other_out):
        for k in range(n):
            put(out, k, *encode(sums[first + k][...] + decode(arrived[k])))
        for k in range(n):
            put(other_out, k, *encode(sums[other_first + k][...]))

    pl.when(c == 0)(lambda: run(0, nxt, n, prv))
    pl.when(c != 0)(lambda: run(n, prv, 0, nxt))


def code_last_kernel(n, *refs):
    sums, (low, high, _, out) = refs[:n], refs[n:]
    for k in range(n):
        level, code = encode(sums[k][...] + decode(low[k]) + decode(high[k]))
        code = jnp.broadcast_to(code, (64, PADDED - HALF))
        for row in range(SIDE):
            rows = slice(16 * row, 16 * (row + 1))
            out[row, k, :, :HALF] = level[rows]
            out[row, k, :, HALF:] = code[rows]


def code_far(sums):
    n = len(sums)
    return pl.pallas_call(
        functools.partial(code_far_kernel, n),
        out_shape=jax.ShapeDtypeStruct((n, 2 * CUT, PADDED), jnp.int16),
        grid=(4,),
        in_specs=[pl.BlockSpec((64, HALF), lambda i: (i, 0))] * n,
        out_specs=pl.BlockSpec((n, 64, PADDED), lambda i: (0, i, 0)),
        compiler_params=VMEM,
        name="code_far",
    )(*sums)


def code_near(sums_next, sums_prev, arrived):
    n = len(sums_next)
    out = jax.ShapeDtypeStruct((n, 2 * CUT, PADDED), jnp.int16)
    block = pl.BlockSpec((n, 64, PADDED), lambda i: (0, i, 0))
    return pl.pallas_call(
        functools.partial(code_near_kernel, n),
        out_shape=(out, out),
        grid=(4,),
        in_specs=[pl.BlockSpec((64, HALF), lambda i: (i, 0))] * (2 * n) + [block],
        out_specs=(block, block),
        compiler_params=VMEM,
        name="code_near",
    )(*sums_next, *sums_prev, arrived)


def code_last(sums, low, high, group, before):
    n = len(sums)
    block = pl.BlockSpec((n, 64, PADDED), lambda i: (0, i, 0))
    return pl.pallas_call(
        functools.partial(code_last_kernel, n),
        out_shape=jax.ShapeDtypeStruct((SIDE * SIDE, 2 * n, 16, PADDED), jnp.int16),
        grid=(4,),
        in_specs=[pl.BlockSpec((64, HALF), lambda i: (i, 0))] * n
        + [block, block, pl.BlockSpec(memory_space=pl.ANY)],
        out_specs=pl.BlockSpec((SIDE, n, 16, PADDED), lambda i: (i, group, 0, 0)),
        input_output_aliases={} if before is None else {n + 2: 0},
        compiler_params=VMEM,
        name="code_last",
    )(*sums, low, high, low if before is None else before)


def finish_kernel(groups, *refs):
    c = lax.axis_index("c")
    got, (virt, occ, out) = refs[: len(groups)], refs[len(groups) :]
    spots = {up: (ref, 2 * k) for ref, group in zip(got, groups) for k, up in enumerate(group)}
    by_zr = one_hot(64, lambda i: ((i // 4) % 4) * 16 + (i // 16) * 4 + i % 4).astype(jnp.float32)
    for ya in range(SIDE):
        for h in range(2):
            parts = []
            for ys in range(SIDE):
                ref, k = spots[(ya - ys) % SIDE]
                parts.append(ref[ys, k + jnp.bitwise_xor(c, h)])
            value = decode(jnp.concatenate(parts, axis=0))
            value = jnp.dot(by_zr, value, precision=lax.Precision.HIGHEST)
            j = 2 * ya + h
            out[:, j * HALF : (j + 1) * HALF] = value / (virt[j : j + 1, :HALF] - occ[...])


def finish(groups, got, virt, occ):
    block = lambda n: pl.BlockSpec((SIDE, n, 16, PADDED), lambda i: (i, 0, 0, 0))
    return pl.pallas_call(
        functools.partial(finish_kernel, groups),
        grid=(SIDE,),
        out_shape=jax.ShapeDtypeStruct((64, SIDE * WIDTH), jnp.float32),
        in_specs=[block(2 * len(group)) for group in groups]
        + [
            pl.BlockSpec((8, PADDED), lambda i: (i, 0)),
            pl.BlockSpec((64, 1), lambda i: (0, 0)),
        ],
        out_specs=pl.BlockSpec((64, WIDTH), lambda i: (0, i)),
        compiler_params=VMEM,
        name="finish",
    )(*got, virt, occ)


def ring_pieces(first, second):
    both = (first, second)
    steps = [ring(piece, axis, shift) for piece, axis, _ in both for shift in (1, -1)]
    steps = lax.optimization_barrier(tuple(steps))
    lows, highs = steps[0::2], steps[1::2]
    fars = []
    for (_, axis, cut), low, high in zip(both, lows, highs):
        fars += [ring(low[:cut], axis, 1), ring(high[cut:], axis, -1)]
    fars = lax.optimization_barrier(tuple(fars))
    return [
        (piece, high, *fars[2 * i : 2 * i + 2], low)
        for i, ((piece, _, _), low, high) in enumerate(zip(both, lows, highs))
    ]


def on_device(amplitudes, integrals, tile_ids, tile_owner, occ_pairs, occ_energy, vir_energy):
    z, y, x, c = (lax.axis_index(name) for name in ALL)
    occ_dev = amplitudes.shape[0]
    sub = occ_dev // (SIDE * SIDE)
    mine = integrals[0]
    other = swap(mine)
    table = make_plan(tile_owner)
    extra = later_rounds(table, mine, other)
    packed = pack(0, table, mine, other, extra)
    first = send(packed)
    last, *leaving = order_amplitudes(table, amplitudes, packed[0])
    prev, far, nxt = send(leaving)
    shard = assemble(table, mine, other, first, extra)
    arrived = jnp.concatenate([far, nxt, prev, last], axis=0)
    arrived, _ = lax.optimization_barrier((arrived, shard))
    shares, pieces = ring_pieces((shard, "y", CUT), (arrived, "z", 2 * occ_dev))
    own, high, far0, far1, low = [(piece, swap(piece)) for piece in shares]
    both = tuple(jnp.concatenate([far0[i], far1[i]], axis=0) for i in range(2))
    blocks = [own, high, both, low]
    by_k = one_hot(256, lambda i: (((i // 4) % 4 - z) % 4) * 64 + (i // 16) * 4 + i % 4)

    def pairs_of(number):
        own, high, far0, far1, low = pieces
        at = lambda p, n: p[n * occ_dev : (n + 1) * occ_dev]
        far = at(far0, number) if number < 2 else at(far1, number - 2)
        whole = jnp.concatenate([at(own, number), at(high, number), far, at(low, number)], axis=0)
        return jnp.dot(by_k, whole, preferred_element_type=jnp.float32).astype(whole.dtype)

    def product(a, b):
        return lax.dot_general(a, b, (((1,), (1,)), ((), ())), preferred_element_type=jnp.float32)

    def sums(number, blocks):
        return [product(pairs[number], b) for b in blocks]

    pairs = [pairs_of(number) for number in range(SIDE)]

    def near_sums(next_pairs, prev_pairs, *blocks):
        return [product(p, b) for p in (next_pairs, prev_pairs) for b in blocks]

    def no_sums(next_pairs, prev_pairs, *blocks):
        return [jnp.zeros((4 * occ_dev, HALF), jnp.float32) for _ in range(2 * len(blocks))]

    groups = ((0, 1), (2, 3))
    parts = [[half for up in group for half in blocks[up]] for group in groups]
    sent = [code_far(sums(0, part)) for part in parts]
    pairs[1], pairs[2], pairs[3], *_ = lax.optimization_barrier((*pairs[1:], *sent))
    far_sums = [part_ring(value, value, "x") for value in sent]
    leaving, behind = [], pairs[1:3]
    for part, arriving in zip(parts, far_sums):
        both = lax.cond(table[1, ROUNDS] >= 0, near_sums, no_sums, *behind, *part)
        leaving.append(code_near(both[: len(part)], both[len(part) :], arriving))
        *behind, _, _ = lax.optimization_barrier((pairs[1], pairs[2], *leaving[-1]))
    near_arrived = [(ring(nxt, "x", 1), ring(prv, "x", -1)) for nxt, prv in leaving]
    pairs[3], *_ = lax.optimization_barrier((pairs[3], *leaving[-1]))
    last_sums = [sums(3, part) for part in parts]
    total = None
    for group, (sums_, arriving) in enumerate(zip(last_sums, near_arrived)):
        total = code_last(sums_, *arriving, group, total)
    got = lax.all_to_all(total, ("z", "y"), split_axis=0, concat_axis=0, tiled=True)
    sent = leaving[-1]
    occ_pairs, occ_energy, vir_energy, _ = lax.optimization_barrier(
        (occ_pairs, occ_energy, vir_energy, sent[0])
    )

    grid = occ_pairs.reshape(SIDE * SIDE, 2 * SIDE, SIDE * SIDE, sub, 2)
    here = lax.dynamic_slice(grid, (0, 2 * x + c, SIDE * z + y, 0, 0), (SIDE * SIDE, 1, 1, sub, 2))
    occ_sum = jnp.sum(jnp.take(occ_energy, here.reshape(occ_dev, 2), axis=0), axis=1)
    per_row = NVIR // TW
    second = jnp.take(vir_energy.reshape(per_row, TW), tile_ids % per_row, axis=0)
    virt_sum = (jnp.take(vir_energy, tile_ids // per_row)[:, None] + second).reshape(8 * SIDE, HALF)
    virt_sum = jnp.pad(virt_sum, ((0, 0), (0, PADDED - HALF)))
    return finish(((0, 1, 2, 3),), (got,), virt_sum, occ_sum[:, None])[None]


def solution(mesh):
    chips = Mesh(mesh.devices.reshape(SIDE, SIDE, SIDE, 2), ALL)
    placed = (P(ALL, None), P(("x", "c"), ("z", "y"), None), P(), P(), P(), P(), P())
    return jax.shard_map(
        on_device, mesh=chips, in_specs=placed, out_specs=P(("z", "y"), ("x", "c"), None), check_vma=False
    )
```
